256 devices in a mesh: seq: 64 (over y, x_hi, z), head: 4 (over x_lo, core).
Axes of the slice: x: 4 (x_hi: 2, x_lo: 2; x = x_hi * 2 + x_lo), y: 4, z: 8, core: 2. Of those that a mesh axis runs over, the one named last changes fastest.
Arguments:
- queries: bfloat16 [8192, 2048], P('seq', 'head'), may hold values from -15 to 15
- key_heads: bfloat16 [8192, 512], P('seq', 'head'), may hold values from -6 to 6
- value_heads: bfloat16 [8192, 512], P('seq', 'head'), may hold values from -6 to 6
- residual: bfloat16 [8192, 3584], P('seq', 'head'), may hold values from -20 to 20
- out_proj: bfloat16 [2048, 3584], P('head'), may hold values from -0.5 to 0.5
- norm_gain: bfloat16 [3584], P('head'), may hold values from 0.099609375 to 1.8984375
- routes: int32 [8192, 4], P('seq'), may hold values from 0 to 63, all different within a row; in each aligned block of 128 rows (0 to 127, 128 to 255, ...) at most 10 rows name the same one
- combine_weight: float32 [8192, 4], P('seq'), may hold values from 0.05 to 1
- gate_up: bfloat16 [64, 3584, 2, 1280], P('seq', None, None, 'head'), may hold values from -0.09375 to 0.09375
- down_proj: bfloat16 [64, 1280, 3584], P('seq', 'head'), may hold values from -0.15625 to 0.15625
Outputs:
- residual_mid: bfloat16 [8192, 3584], P('seq', 'head')
- expert_out: bfloat16 [8192, 3584], P('seq', 'head')
The draws below stay inside these ranges and needn't reach their ends.
Inputs may be any that keep to these rules, and one draw needn't show every extreme that they name: `routes`: in the rows of one index of seq (128 positions) no expert is named more than 10 times, and this bound is reached in every draw.
All inputs are finite; a program needn't handle non-finite values.
Results may differ from the reference program's by a relative error of at most 0.03.
Values may be sent and summed in bfloat16 or wider, within the bound.
A program may use at most 128 MiB of HBM per device.

```python
import math
import jax
import jax.numpy as jnp
import numpy as np
from jax import lax

D = 3584
HD = 128
QHEADS = 16
KVHEADS = 4
EXPERTS = 64
TOPK = 4
EH = 1280
TOK = 128
SEQ_LEN = 8192
CAP = 10
N_SEQ = 64
N_HEAD = 4


def draw_key_heads(key, part):
    key = jax.random.fold_in(key, 3)
    sample = jnp.clip(jax.random.normal(key, (SEQ_LEN, KVHEADS, HD), jnp.float32), -6.0, 6.0)
    return sample.reshape(SEQ_LEN, KVHEADS * HD).astype(jnp.bfloat16)


def draw_queries(key, part):
    key = jax.random.fold_in(key, 5)
    sample = jnp.clip(2.5 * jax.random.normal(key, (SEQ_LEN, QHEADS, HD), jnp.float32), -15.0, 15.0)
    return sample.reshape(SEQ_LEN, QHEADS * HD).astype(jnp.bfloat16)


def draw_residual(key, part):
    key = jax.random.fold_in(key, 7)
    noise_key, column_key = jax.random.split(key, 2)
    columns = jnp.arange(D)
    spread = jax.random.uniform(column_key, (D,), jnp.float32)
    column_scale = 10.0 ** (((columns * 4 // D).astype(jnp.float32) + spread) / 4.0 - 0.5)
    noise = jnp.clip(jax.random.normal(noise_key, (SEQ_LEN, D), jnp.float32), -6.0, 6.0)
    return (noise * column_scale[None, :]).astype(jnp.bfloat16)


def level_of(own_key, shape, cuts, least, largest):
    factor_of, own = 1.0, jax.random.fold_in(own_key, 6)
    for dim, blocks in cuts:
        draws = jnp.exp(jax.random.uniform(jax.random.fold_in(own, dim), (blocks,), jnp.float32, least / len(cuts), largest / len(cuts)))
        factor_of = factor_of * jnp.repeat(draws, shape[dim] // blocks).reshape([-1 if axis == dim else 1 for axis in range(len(shape))])
    return factor_of


def routed_block(stream_key, own, number, rows, count, top, reach, skew):
    order = jax.random.permutation(stream_key, count)
    packed, common = load_shares(count, rows * top, reach, skew, True), load_shares(count, rows * top, reach, skew, False)
    places = jnp.arange(count)

    def named(tallies, rotation):
        used = int((tallies > 0).sum())
        fixed = max(1, used // 4)
        passed = fixed + (places - fixed + rotation * (used - fixed)) % max(1, count - fixed)
        return jnp.zeros((count,), jnp.int32).at[order[jnp.where(places < fixed, places, passed)]].set(jnp.asarray(tallies, jnp.int32))

    tallies = jnp.where(number % 4 == 0, named(packed, number // 4), named(common, number - number // 4 - 1))
    mixed = jax.random.permutation(jax.random.fold_in(own, 3), count)
    source_of, sink = mixed[0:count // 2 * 2:2], mixed[1:count // 2 * 2:2]
    slack = jnp.minimum(tallies[source_of] - 1, reach - tallies[sink]) // 2
    slack = jnp.where((source_of == order[0]) | (sink == order[0]) | (tallies[sink] == 0), 0, jnp.maximum(slack, 0))
    passed = jax.random.randint(jax.random.fold_in(own, 4), (count // 2,), 0, 1 << 20) % (slack + 1)
    tallies = tallies.at[source_of].add(-passed).at[sink].add(passed)
    members = jnp.searchsorted(jnp.cumsum(tallies), jnp.arange(rows * top), side="right").astype(jnp.int32)
    grid = members.reshape(top, rows).T
    grid = grid[jax.random.permutation(jax.random.fold_in(own, 1), rows)]
    rotation = jax.random.randint(jax.random.fold_in(own, 2), (rows, 1), 0, top)
    return jnp.take_along_axis(grid, (jnp.arange(top)[None, :] + rotation) % top, axis=1)


def load_shares(amount, total, most, slope, full):
    loads = [(1 << 20) // math.isqrt(rank ** slope) + 1 for rank in range(1, amount + 1)]
    largest = most if full else min(most, max(-(-total // amount), total * loads[0] // sum(loads)))
    least = 1 if total - largest >= amount - 1 else 0
    given, rest = [largest] + [least] * (amount - 1), total - largest - least * (amount - 1)
    while rest > 0:
        candidates = [i for i in range(1, amount) if given[i] < largest] or [i for i in range(1, amount) if given[i] < most]
        pool, budget = sum([loads[i] for i in candidates]), rest
        for i in candidates:
            more = min(most - given[i], max(1, budget * loads[i] // pool), rest)
            given[i] = given[i] + more
            rest = rest - more
    return np.array(given)


def gaussian(rng, shape, width, most, cuts=(), kind=jnp.bfloat16):
    loudness = level_of(rng, shape, cuts, -0.22, 0.18) if cuts else 1.0
    drawn = jax.random.normal(rng, shape, jnp.float32) * width * loudness
    return jnp.minimum(jnp.maximum(drawn, -most), most).astype(kind)


def setup_inputs(seed: int = 0) -> dict:
    keys = jax.random.split(jax.random.key(seed), 11)
    queries = draw_queries(jax.random.fold_in(keys[10], 71), 0)
    key_heads = draw_key_heads(jax.random.fold_in(keys[10], 71), 0)
    value_heads = gaussian(keys[2], (SEQ_LEN, KVHEADS * HD), 1.0, 6.0, ((0, 64), (1, 4)))
    residual = draw_residual(jax.random.fold_in(keys[10], 71), 0)
    out_proj = gaussian(keys[4], (QHEADS * HD, D), (QHEADS * HD // 16) ** -0.5, 0.5, ((0, 4),))
    norm_gain = jnp.clip(1.0 + 0.18 * jax.random.normal(keys[5], (D,), jnp.float32), 0.099609375, 1.8984375).astype(jnp.bfloat16)
    routes_keys = jax.random.split(jax.random.fold_in(keys[6], 1), SEQ_LEN // TOK)
    routes_turns = jax.random.permutation(jax.random.fold_in(keys[6], 3), SEQ_LEN // TOK)
    routes = jax.vmap(lambda own, number: routed_block(jax.random.fold_in(keys[6], 2), own, number, TOK, EXPERTS, TOPK, CAP, 2))(routes_keys, routes_turns).reshape((SEQ_LEN, TOPK))
    combine_weight = jnp.clip(jnp.exp(math.log(1.0) - 2.9957323 * jax.random.uniform(keys[7], (SEQ_LEN, TOPK), jnp.float32) ** level_of(keys[7], (SEQ_LEN, TOPK), ((0, 64),), -0.2, 0.2)), 0.05, 1.0)
    gate_up = gaussian(keys[8], (EXPERTS, D, 2, EH), D ** -0.5, 0.09375, ((0, 64), (3, 4)))
    down_proj = gaussian(keys[9], (EXPERTS, EH, D), EH ** -0.5, 0.15625, ((0, 64), (1, 4)))
    return dict(queries=queries, key_heads=key_heads, value_heads=value_heads, residual=residual, out_proj=out_proj, norm_gain=norm_gain, routes=routes, combine_weight=combine_weight, gate_up=gate_up, down_proj=down_proj)


epsilon = 1e-06

def attention_block(query_block, keys_whole, values_whole):
    scores = jnp.einsum('qkgd,jkd->kgqj', query_block, keys_whole, precision=lax.Precision.HIGHEST) * (1.0 / math.sqrt(HD))
    row_max = lax.optimization_barrier(jnp.max(scores, axis=3, keepdims=True))
    weights = jnp.exp(scores - row_max)
    totals = lax.optimization_barrier(jnp.sum(weights, axis=3))
    rounded = lax.optimization_barrier(weights.astype(jnp.bfloat16)).astype(jnp.float32)
    summed = jnp.einsum('kgqj,jkd->kgqd', rounded, values_whole, precision=lax.Precision.HIGHEST)
    attended = summed / totals[..., None]
    return jnp.transpose(attended, (2, 0, 1, 3))

def reference(queries, key_heads, value_heads, residual, out_proj, norm_gain, routes, combine_weight, gate_up, down_proj):
    group_size = QHEADS // KVHEADS
    query_four = queries.astype(jnp.float32).reshape(SEQ_LEN, KVHEADS, group_size, HD)
    keys_whole = key_heads.astype(jnp.float32).reshape(SEQ_LEN, KVHEADS, HD)
    values_whole = value_heads.astype(jnp.float32).reshape(SEQ_LEN, KVHEADS, HD)
    block_size = math.gcd(SEQ_LEN, 256)
    blocks = query_four.reshape(SEQ_LEN // block_size, block_size, KVHEADS, group_size, HD)

    def one_block(query_block):
        return attention_block(query_block, keys_whole, values_whole)
    attended = lax.map(one_block, blocks).reshape(SEQ_LEN, QHEADS * HD).astype(jnp.bfloat16)
    projected = jnp.dot(attended, out_proj, preferred_element_type=jnp.float32)
    residual_mid = (residual.astype(jnp.float32) + projected).astype(jnp.bfloat16)
    mid_float = residual_mid.astype(jnp.float32)
    mean_square = lax.optimization_barrier(jnp.mean(mid_float * mid_float, axis=1, keepdims=True))
    normed = (mid_float * lax.rsqrt(mean_square + epsilon) * norm_gain.astype(jnp.float32)).astype(jnp.bfloat16)
    flat_routes = routes.reshape(N_SEQ, TOK * TOPK)
    onehot = (flat_routes[:, :, None] == jnp.arange(EXPERTS, dtype=jnp.int32)[None, None, :]).astype(jnp.int32)
    slot_index = lax.optimization_barrier(jnp.sum((jnp.cumsum(onehot, axis=1) - onehot) * onehot, axis=2)).astype(jnp.int32)
    source = jnp.broadcast_to(jnp.arange(N_SEQ, dtype=jnp.int32)[:, None], (N_SEQ, TOK * TOPK))
    token_id = (source * TOK + jnp.arange(TOK * TOPK, dtype=jnp.int32)[None, :] // TOPK).astype(jnp.int32)
    slot_table = jnp.full((EXPERTS, N_SEQ, CAP), SEQ_LEN, jnp.int32).at[flat_routes, source, slot_index].set(token_id)
    weight_table = jnp.zeros((EXPERTS, N_SEQ, CAP), jnp.float32).at[flat_routes, source, slot_index].set(combine_weight.astype(jnp.float32).reshape(N_SEQ, TOK * TOPK))
    padded = jnp.concatenate([normed, jnp.zeros((1, D), jnp.bfloat16)], axis=0)
    quarter = EH // N_HEAD

    def per_expert(accumulated, inputs):
        gate_up_one, down_one, table_one, weight_one = inputs
        positions = table_one.reshape(-1)
        gathered = padded[positions]
        gate_and_up = jnp.dot(gathered, gate_up_one.reshape(D, 2 * EH), preferred_element_type=jnp.float32)
        activated = (jax.nn.silu(gate_and_up[:, :EH]) * gate_and_up[:, EH:]).astype(jnp.bfloat16)
        act_three = activated.astype(jnp.float32).reshape(-1, N_HEAD, quarter)
        down_three = down_one.astype(jnp.float32).reshape(N_HEAD, quarter, D)
        partials = jnp.einsum('rjf,jfd->rjd', act_three, down_three, precision=lax.Precision.HIGHEST)
        partials = lax.optimization_barrier(partials.astype(jnp.bfloat16)).astype(jnp.float32)
        result = lax.optimization_barrier(lax.optimization_barrier(jnp.sum(partials, axis=1)).astype(jnp.bfloat16)).astype(jnp.float32)
        accumulated = accumulated.at[positions].add(weight_one.reshape(-1)[:, None] * result)
        return (accumulated, None)
    start_total = jnp.zeros((SEQ_LEN + 1, D), jnp.float32)
    accumulated, unused = lax.scan(per_expert, start_total, (gate_up, down_proj, slot_table, weight_table))
    expert_out = accumulated[:SEQ_LEN].astype(jnp.bfloat16)
    return (residual_mid, expert_out)
```

```python
import math

import jax
import jax.numpy as jnp
from jax import lax
from jax.experimental import pallas as pl
from jax.experimental.pallas import tpu as pltpu
from jax.sharding import PartitionSpec as P

D = 3584
HD = 128
TOK = 128
QUARTER = 896
HALF = 1792
HID = 320
ROWS_A = 80
SLOT_ROWS = 144
GROUP = 8
GROUPS = 4
GROUP_ROWS = 80
EPSILON = 1e-06
SCALE2 = math.log2(math.e) / math.sqrt(HD)
MESH = pl.DeviceIdType.MESH
F32 = jnp.float32
BF16 = jnp.bfloat16


def dot(a, b):
    return jnp.dot(a, b, preferred_element_type=F32)


def dot_nt(a, b):
    return lax.dot_general(a, b, (((1,), (1,)), ((), ())), preferred_element_type=F32)


def iota(shape, dim):
    return lax.broadcasted_iota(jnp.int32, shape, dim)


def kernel(
    q_ref,
    k_ref,
    v_ref,
    residual_ref,
    out_proj_ref,
    gain_ref,
    routes_ref,
    weight_ref,
    gate_up_ref,
    down_ref,
    mid_ref,
    out_ref,
    kv,
    qr,
    acc,
    row_max,
    part_send,
    part_recv,
    stat_send,
    stat_recv,
    att,
    wo,
    rs_send,
    rs_recv,
    gains,
    mid_half,
    squares,
    wc,
    onehot,
    perm,
    ymat,
    send_buf,
    xbuf,
    xmat,
    gu,
    wd,
    po_send,
    po_recv,
    po_own,
    ret_send,
    ret,
    rmat,
    comb_send,
    comb_recv,
    ra,
    rb,
    rd,
    rp,
    rpo,
    spo,
    rr,
    sa,
    sb,
    sd,
    sp,
    sr,
    misc_send,
    misc_recv,
    weight_send,
    weight_recv,
    weight_local,
):
    seq, head = lax.axis_index("seq"), lax.axis_index("head")
    y, z = lax.div(seq, 16), lax.rem(seq, 8)
    xh = lax.rem(lax.div(seq, 8), 2)
    xl, core = lax.div(head, 2), lax.rem(head, 2)
    other = 1 - core
    z_even, y_even, core_zero = lax.rem(z, 2) == 0, lax.rem(y, 2) == 0, core == 0
    my_kv = z * 4 + y
    my_j = y * 8 + z
    far_h, far_l = (xh + core) % 2, (xl + core) % 2
    half_in = far_l

    def dev(y_, xh_, z_, xl_, core_):
        return {"seq": (y_ * 2 + xh_) * 8 + z_, "head": xl_ * 2 + core_}

    partner = dev(y, xh, z, xl, other)
    pair = dev(y, xh, z, 1 - xl, core)
    diagonal = dev(y, xh, z, 1 - xl, other)
    twin = dev(y, 1 - xh, z, xl, core)

    def wrap(a, n):
        return lax.rem(a + n, n)

    yp, ym, y2 = wrap(y + 1, 4), wrap(y - 1, 4), wrap(y + 2, 4)
    zp, zm = wrap(z + 1, 8), wrap(z - 1, 8)

    def far(j):
        return dev(lax.div(j, 8), far_h, lax.rem(j, 8), far_l, core)

    barrier = pltpu.get_barrier_semaphore()

    def greet(device):
        pl.semaphore_signal(barrier, inc=1, device_id=device, device_id_type=MESH)

    for device in (
        dev(yp, xh, z, xl, core),
        dev(ym, xh, z, xl, core),
        dev(y, xh, zp, xl, core),
        dev(y, xh, zm, xl, core),
        twin,
        partner,
        pair,
        diagonal,
    ):
        greet(device)

    def greet_far(i, carry):
        greet(far(lax.rem(my_j + i, 32)))
        return carry

    lax.fori_loop(1, 32, greet_far, 0)

    @pl.when(core == 1)
    def _():
        greet(far(my_j))

    for j in range(4):
        qr[j * TOK : (j + 1) * TOK, :] = q_ref[:, j * HD : (j + 1) * HD]
    kv[:, :, 256:384] = jnp.ones((32, TOK, HD), BF16)
    kv[my_kv, :, 0:128] = k_ref[...]
    kv[my_kv, :, 128:256] = v_ref[...]
    gains[core, :, :] = jnp.broadcast_to(gain_ref[...].astype(F32), (8, QUARTER))
    pl.semaphore_wait(barrier, 39 + core)

    def rcopy(src, dst, send, recv, device):
        return pltpu.make_async_remote_copy(
            src_ref=src,
            dst_ref=dst,
            send_sem=send,
            recv_sem=recv,
            device_id=device,
            device_id_type=MESH,
        )

    def part_a(b):
        return kv.at[b, pl.ds(0, ROWS_A), pl.ds(0, 256)]

    def part_b(b):
        return kv.at[b, pl.ds(ROWS_A, TOK - ROWS_A), pl.ds(0, 256)]

    def send_a(zb, yb, y_, z_):
        b = zb * 4 + yb
        rcopy(part_a(b), part_a(b), sa, ra.at[b], dev(y_, xh, z_, xl, core)).start()

    def send_b(zb, yb, y_, z_):
        b = zb * 4 + yb
        rcopy(part_b(b), part_b(b), sb, rb.at[b], dev(y_, xh, z_, xl, core)).start()

    def wait_a(zb, yb):
        b = zb * 4 + yb
        pltpu.make_async_copy(part_a(b), part_a(b), ra.at[b]).wait()

    def wait_b(zb, yb):
        b = zb * 4 + yb
        pltpu.make_async_copy(part_b(b), part_b(b), rb.at[b]).wait()

    send_a(z, y, y, zp)
    send_a(z, y, y, zm)
    send_b(z, y, yp, z)
    send_b(z, y, ym, z)
    send_a(z, y, yp, z)
    send_a(z, y, ym, z)
    send_b(z, y, y, zp)
    send_b(z, y, y, zm)
    q_copy = rcopy(
        qr.at[pl.ds(0, 512)], qr.at[pl.ds(512, 512)], misc_send.at[0], misc_recv.at[0], twin
    )
    q_copy.start()
    gain_copy = rcopy(gains.at[core], gains.at[core], misc_send.at[1], misc_recv.at[1], partner)
    gain_copy.start()

    wo_copies = []
    for hf in range(2):
        mine = pl.ds(pl.multiple_of((hf * 2 + core) * QUARTER, 128), QUARTER)
        theirs = pl.ds(pl.multiple_of((hf * 2 + other) * QUARTER, 128), QUARTER)
        wo_copies.append(
            rcopy(
                out_proj_ref.at[:, theirs],
                wo.at[core, hf],
                weight_send.at[hf],
                weight_recv.at[hf],
                partner,
            )
        )
        wo_copies[-1].start()
        wo_copies.append(
            pltpu.make_async_copy(out_proj_ref.at[:, mine], wo.at[core, hf], weight_local.at[hf])
        )
    for copy in wo_copies[1::2]:
        copy.start()
    ffn_copies = []
    for n, (src, dst) in enumerate(((gate_up_ref, gu), (down_ref, wd))):
        remote = rcopy(
            src, dst.at[core], weight_send.at[2 + n], weight_recv.at[2 + n], partner
        )
        local = pltpu.make_async_copy(src, dst.at[core], weight_local.at[2 + n])
        remote.start()
        local.start()
        ffn_copies += [remote, local]

    acc[...] = jnp.zeros((1024, 256), F32)
    row_max[...] = jnp.full((1024, HD), -1e30, F32)

    lane = iota((1, 384), 1)
    main = lane < 256
    extra = lane - 256
    j_row = jnp.where(main, lax.shift_right_logical(lane, 3), lax.shift_right_logical(jnp.maximum(extra, 0), 1))
    s_row = jnp.where(main, lane & 7, 8 + (extra & 1))
    e_row = lax.shift_right_logical(j_row, 3) * 16 + far_h * 8 + (j_row & 7)
    e_row = jnp.where(j_row < 32, e_row, -1)
    named = jnp.zeros((TOK, 384), F32)
    weight = jnp.zeros((TOK, 384), F32)
    for k in range(4):
        same = routes_ref[:, k : k + 1] == e_row
        named = jnp.where(same, 1.0, named)
        weight = jnp.where(same, weight_ref[:, k : k + 1], weight)
    earlier = jnp.where(iota((TOK, TOK), 1) < iota((TOK, TOK), 0), 1.0, 0.0).astype(BF16)
    count = dot(earlier, named.astype(BF16))
    taken = jnp.where(count == s_row.astype(F32), named, 0.0)
    weight = weight * taken
    high = weight.astype(BF16)
    wc[0] = high
    wc[1] = (weight - high.astype(F32)).astype(BF16)
    onehot[...] = taken.T
    for which in range(2):
        o, i = iota((256, 256), which), iota((256, 256), 1 - which)
        rem = o & 31
        source = lax.shift_right_logical(rem, 1) * 16 + lax.shift_right_logical(o, 5) * 2 + (rem & 1)
        perm[which] = jnp.where((source == i) & (rem < 28), 1.0, 0.0).astype(BF16)
    rmat[...] = jnp.zeros((384, HALF), BF16)

    eye = iota((TOK, TOK), 0) == iota((TOK, TOK), 1)

    def to_row(column):
        return jnp.sum(jnp.where(eye, column, 0.0), axis=0, keepdims=True)

    def to_column(row):
        return jnp.sum(jnp.where(eye, row, 0.0), axis=1, keepdims=True)

    def flash(zb, first, count):
        block = kv[pl.ds(zb * 4, 4)]
        keys = block[:, :, 0:128].reshape(512, HD)
        values = block[:, :, 128:384].reshape(512, 256)

        def tile(t, carry):
            rows = pl.ds(pl.multiple_of(first + t * 256, 256), 256)
            scores = dot_nt(qr[rows, :], keys)
            old = row_max[rows, :]
            new = jnp.maximum(old, jnp.max(scores, axis=1, keepdims=True))
            p = jnp.exp2((scores - new[:, 0:1]) * SCALE2).astype(BF16)
            fade = jnp.exp2((old - new) * SCALE2)
            add = dot(p, values)
            acc[rows, 0:128] = acc[rows, 0:128] * fade + add[:, 0:128]
            acc[rows, 128:256] = acc[rows, 128:256] * fade + add[:, 128:256]
            row_max[rows, :] = new
            return carry

        lax.fori_loop(0, count // 256, tile, 0)

    def y_stage(zb):
        even = lax.rem(zb, 2) == 0
        wait_a(zb, ym)

        @pl.when(even)
        def _():
            send_a(zb, ym, yp, z)

        wait_a(zb, yp)

        @pl.when(jnp.logical_not(even))
        def _():
            send_a(zb, yp, ym, z)

    for yb, forward, to in ((ym, z_even, yp), (yp, jnp.logical_not(z_even), ym)):
        wait_b(z, yb)
        send_b(z, yb, y, zp)
        send_b(z, yb, y, zm)

        @pl.when(forward)
        def _():
            send_b(z, yb, to, z)

    y_stage(z)
    wait_b(z, y2)
    send_b(z, y2, y, zp)
    send_b(z, y2, y, zm)

    def z_stage(d):
        for zb, to, parity in ((wrap(z - d, 8), zp, 0), (wrap(z + d, 8), zm, 1)):
            wait_a(zb, y)
            goes = (d < 3) | ((d == 3) & (lax.rem(y, 2) == parity))

            @pl.when(goes)
            def _():
                send_a(zb, y, y, to)

            send_a(zb, y, yp, z)
            send_a(zb, y, ym, z)

            def each(yb, carry):
                wait_b(zb, yb)

                @pl.when((d < 3) | ((d == 3) & (lax.rem(yb, 2) == parity)))
                def _():
                    send_b(zb, yb, y, to)

                return carry

            lax.fori_loop(0, 4, each, 0)

    def step(d, carry):
        z_stage(d)

        @pl.when(d == 1)
        def _():
            q_copy.wait_recv()
            wait_a(z, y2)
            flash(z, 0, 1024)

        @pl.when(d > 1)
        def _():
            for zb in (wrap(z - d + 1, 8), wrap(z + d - 1, 8)):
                wait_a(zb, y2)
                flash(zb, 0, 1024)

        y_stage(wrap(z - d, 8))
        y_stage(wrap(z + d, 8))
        return carry

    lax.fori_loop(1, 4, step, 0)
    zf = wrap(z + 4, 8)
    wait_a(zf, y)
    send_a(zf, y, yp, z)
    send_a(zf, y, ym, z)
    for zb in (wrap(z - 3, 8), wrap(z + 3, 8)):
        wait_a(zb, y2)
        flash(zb, 0, 1024)
    y_stage(zf)
    wait_a(zf, y2)
    for yb in range(4):
        wait_b(zf, yb)

    flash(zf, 512, 512)
    for j in range(4):
        rows = pl.ds(512 + j * TOK, TOK)
        total = acc[rows, 128:256]
        part_send[j * TOK : (j + 1) * TOK, :] = (acc[rows, 0:128] / total).astype(BF16)
        stat_send[j : j + 1, :] = to_row(row_max[rows, :] * SCALE2 + jnp.log2(total))
    stat_send[4:8, :] = jnp.zeros((4, TOK), F32)
    part_copy = rcopy(part_send, part_recv, misc_send.at[2], misc_recv.at[2], twin)
    stat_copy = rcopy(stat_send, stat_recv, misc_send.at[3], misc_recv.at[3], twin)
    part_copy.start()
    stat_copy.start()
    flash(zf, 0, 512)
    part_copy.wait_recv()
    stat_copy.wait_recv()
    for j in range(4):
        rows = slice(j * TOK, (j + 1) * TOK)
        total = acc[rows, 128:256]
        own = acc[rows, 0:128] / total
        own_stat = row_max[rows, :] * SCALE2 + jnp.log2(total)
        their_stat = to_column(stat_recv[j : j + 1, :])
        own_share = 1.0 / (1.0 + jnp.exp2(their_stat - own_stat))
        their_share = 1.0 / (1.0 + jnp.exp2(own_stat - their_stat))
        att[core, :, rows] = (
            own * own_share + part_recv[rows, :].astype(F32) * their_share
        ).astype(BF16)
    att_copy = rcopy(att.at[core], att.at[core], misc_send.at[4], misc_recv.at[4], partner)
    att_copy.start()
    for copy in wo_copies[0::2]:
        copy.wait_recv()
    for copy in wo_copies[1::2]:
        copy.wait()
    gain_copy.wait_recv()
    att_copy.wait_recv()

    def project(hf):
        return dot(att[0], wo[0, hf]) + dot(att[1], wo[1, hf])

    rs_send[...] = project(1 - xl).astype(BF16)
    rs_copy = rcopy(rs_send, rs_recv, misc_send.at[5], misc_recv.at[5], pair)
    rs_copy.start()
    own = project(xl) + residual_ref[...].astype(F32)
    rs_copy.wait_recv()
    middle = (own + rs_recv[...].astype(F32)).astype(BF16)
    mid_half[core, :, :] = middle
    mid_copy = rcopy(
        mid_half.at[core], mid_half.at[core], misc_send.at[6], misc_recv.at[6], partner
    )
    mid_copy.start()
    mid_ref[...] = middle
    mid_float = middle.astype(F32)
    squares[head] = jnp.broadcast_to(
        to_row(jnp.sum(mid_float * mid_float, axis=1, keepdims=True)), (8, TOK)
    )
    square_copies = [
        rcopy(squares.at[head], squares.at[head], misc_send.at[7 + n], misc_recv.at[7 + n], device)
        for n, device in enumerate((partner, pair, diagonal))
    ]
    for copy in square_copies:
        copy.start()
    mid_copy.wait_recv()
    hot = onehot[...]
    hot16 = hot.astype(BF16)
    for c in range(2):
        ymat[:, c * QUARTER : (c + 1) * QUARTER] = dot(hot16, mid_half[c])
    for copy in square_copies:
        copy.wait_recv()
    total = squares[0, 0:1] + squares[1, 0:1] + squares[2, 0:1] + squares[3, 0:1]
    inverse = lax.rsqrt(total / D + EPSILON)
    row_scale = jnp.sum(hot * inverse, axis=1, keepdims=True)

    def lane_block(c):
        return slice(c * 128, (c + 1) * 128)

    def scaled(rows, c):
        q, inner = c // 7, c % 7
        return ymat[rows, lane_block(c)] * row_scale[rows] * gains[q, 0:1, lane_block(inner)]

    for c in range(0, 14, 2):
        both = [scaled(slice(0, 256), c + n).reshape(32, 8, 128) for n in range(2)]
        send_buf[:, c * 8 : c * 8 + 16, :] = jnp.concatenate(both, axis=1).astype(BF16)
    for g in range(4):
        rows = slice(256 + 16 * g, 272 + 16 * g)
        stack = jnp.concatenate(
            [scaled(rows, c).astype(BF16) for c in range(14)] + [jnp.zeros((32, 128), BF16)], axis=0
        )
        send_buf[8 * g : 8 * g + 8, 112:144, :] = (
            dot(perm[0], stack).reshape(8, 32, 128).astype(BF16)
        )

    def exchange(buffer, place, send, recv, first, count):
        def one(i, carry):
            j = lax.rem(my_j + i, 32)
            rcopy(buffer.at[j], place(), send, recv.at[my_j], far(j)).start()
            return carry

        lax.fori_loop(first, count, one, 0)

    def landing():
        return xbuf.at[xl, my_j]

    @pl.when(core_zero)
    def _():
        pltpu.make_async_copy(send_buf.at[my_j], xbuf.at[xl, my_j], rd.at[my_j]).start()

    @pl.when(core == 1)
    def _():
        rcopy(send_buf.at[my_j], landing(), sd, rd.at[my_j], far(my_j)).start()

    exchange(send_buf, landing, sd, rd, 1, 32)

    for copy in ffn_copies[0::2]:
        copy.wait_recv()
    for copy in ffn_copies[1::2]:
        copy.wait()

    def source(i):
        return wrap(my_j - i, 32)

    def forward(g):
        def one(n, carry):
            s = source(g * GROUP + n)
            block = xbuf.at[half_in, s]
            pltpu.make_async_copy(block, block, rd.at[s]).wait()
            rcopy(block, block, sp, rp.at[s], pair).start()
            return carry

        lax.fori_loop(0, GROUP, one, 0)

    def gather_rows(g):
        def await_pair(n, carry):
            s = source(g * GROUP + n)
            block = xbuf.at[1 - half_in, s]
            pltpu.make_async_copy(block, block, rp.at[s]).wait()
            return carry

        lax.fori_loop(0, GROUP, await_pair, 0)
        for half in range(2):
            for p in range(GROUP // 2):
                both = [
                    xbuf[half, source(g * GROUP + 2 * p + n), 0:112, :]
                    .astype(F32)
                    .reshape(14, 8, 128)
                    for n in range(2)
                ]
                rows = jnp.concatenate(both, axis=1).astype(BF16)
                for c in range(14):
                    xmat[16 * p : 16 * p + 16, lane_block(half * 14 + c)] = rows[c]
            stack = jnp.concatenate(
                [xbuf[half, source(g * GROUP + n), 112:144, :] for n in range(GROUP)], axis=0
            )
            rows = dot(perm[1], stack).astype(BF16)
            for c in range(14):
                xmat[64:80, lane_block(half * 14 + c)] = rows[16 * c : 16 * c + 16]

    def experts(g):
        x = xmat[...]
        parts = []
        for c in range(2):
            hidden = dot(x, gu[c])
            gate, up = hidden[:, :HID], hidden[:, HID:]
            parts.append((gate / (1.0 + jnp.exp(-gate)) * up).astype(BF16))

        def result(half, n):
            columns = pl.ds(pl.multiple_of(half * HALF + n * QUARTER, 128), QUARTER)
            return dot(parts[0], wd[0, :, columns]) + dot(parts[1], wd[1, :, columns])

        for n in range(2):
            po_send[g, :, n * QUARTER : (n + 1) * QUARTER] = result(1 - half_in, n).astype(BF16)
        rcopy(po_send.at[g], po_recv.at[g], spo.at[g], rpo.at[g], pair).start()
        for n in range(2):
            po_own[g, :, n * QUARTER : (n + 1) * QUARTER] = result(half_in, n)

    def give_back(g):
        pltpu.make_async_copy(po_recv.at[g], po_recv.at[g], rpo.at[g]).wait()
        first = pl.multiple_of(g * GROUP, GROUP)

        def summed(rows, c):
            return po_own[g, rows, lane_block(c)] + po_recv[g, rows, lane_block(c)].astype(F32)

        for c in range(0, 14, 2):
            both = [summed(slice(0, 64), c + n).reshape(8, 8, 128) for n in range(2)]
            ret_send[pl.ds(first, 8), c * 8 : c * 8 + 16, :] = jnp.concatenate(both, axis=1).astype(
                BF16
            )
        stack = jnp.concatenate(
            [summed(slice(64, 80), c).astype(BF16) for c in range(14)]
            + [jnp.zeros((32, 128), BF16)],
            axis=0,
        )
        ret_send[pl.ds(first, 8), 112:144, :] = dot(perm[0], stack).reshape(8, 32, 128).astype(BF16)

        def one(n, carry):
            i = g * GROUP + n
            s = source(i)

            @pl.when(core_zero & (i == 0))
            def _():
                pltpu.make_async_copy(ret_send.at[i], ret.at[my_j], rr.at[my_j]).start()

            @pl.when(jnp.logical_not(core_zero & (i == 0)))
            def _():
                rcopy(ret_send.at[i], ret.at[my_j], sr, rr.at[my_j], far(s)).start()

            return carry

        lax.fori_loop(0, GROUP, one, 0)

    forward(0)

    def turn(g, carry):
        @pl.when(g < GROUPS - 1)
        def _():
            forward(g + 1)

        gather_rows(g)
        experts(g)

        @pl.when(g > 0)
        def _():
            give_back(g - 1)

        return carry

    lax.fori_loop(0, GROUPS, turn, 0)
    give_back(GROUPS - 1)

    def await_return(i, carry):
        j = lax.rem(my_j + i, 32)
        pltpu.make_async_copy(ret.at[j], ret.at[j], rr.at[j]).wait()
        return carry

    lax.fori_loop(0, 32, await_return, 0)
    for c in range(0, 14, 2):
        both = ret[:, c * 8 : c * 8 + 16, :].astype(F32)
        for n in range(2):
            rmat[0:256, lane_block(c + n)] = both[:, 8 * n : 8 * n + 8].reshape(256, 128).astype(BF16)
    for g in range(4):
        stack = ret[8 * g : 8 * g + 8, 112:144, :].reshape(256, 128)
        rows = dot(perm[1], stack).astype(BF16)
        for c in range(14):
            rmat[256 + 16 * g : 272 + 16 * g, lane_block(c)] = rows[16 * c : 16 * c + 16]

    def combined(which):
        columns = pl.ds(pl.multiple_of(which * QUARTER, 128), QUARTER)
        rows = rmat[:, columns]
        return dot(wc[0], rows) + dot(wc[1], rows)

    comb_send[...] = combined(other).astype(BF16)
    comb_copy = rcopy(comb_send, comb_recv, misc_send.at[10], misc_recv.at[10], partner)
    comb_copy.start()
    own = combined(core)
    comb_copy.wait_recv()
    out_ref[...] = (own + comb_recv[...].astype(F32)).astype(BF16)

    for copy in (
        [q_copy, gain_copy, part_copy, stat_copy, att_copy, rs_copy, mid_copy, comb_copy]
        + square_copies
        + wo_copies[0::2]
        + ffn_copies[0::2]
    ):
        copy.wait_send()
    for g in range(GROUPS):
        pltpu.make_async_copy(po_send.at[g], po_send.at[g], spo.at[g]).wait()

    def drain(ref, sem):
        pltpu.make_async_copy(ref, ref, sem).wait()

    drain(kv.at[pl.ds(0, 31), pl.ds(0, ROWS_A), pl.ds(0, 256)], sa)
    drain(kv.at[pl.ds(0, 31), pl.ds(ROWS_A, TOK - ROWS_A), pl.ds(0, 256)], sb)
    drain(xbuf.at[0], sp)
    for sem in (sd, sr):

        @pl.when(core_zero)
        def _():
            drain(send_buf.at[pl.ds(0, 31)], sem)

        @pl.when(core == 1)
        def _():
            drain(send_buf, sem)


def body(
    queries,
    key_heads,
    value_heads,
    residual,
    out_proj,
    norm_gain,
    routes,
    combine_weight,
    gate_up,
    down_proj,
):
    vmem = pl.BlockSpec(memory_space=pltpu.VMEM)
    hbm = pl.BlockSpec(memory_space=pl.ANY)
    dma = pltpu.SemaphoreType.DMA
    return pl.pallas_call(
        kernel,
        out_shape=(
            jax.ShapeDtypeStruct((TOK, QUARTER), BF16),
            jax.ShapeDtypeStruct((TOK, QUARTER), BF16),
        ),
        in_specs=[vmem, vmem, vmem, vmem, hbm, vmem, vmem, vmem, hbm, hbm],
        out_specs=(vmem, vmem),
        scratch_shapes=[
            pltpu.VMEM((32, TOK, 384), BF16),
            pltpu.VMEM((1024, HD), BF16),
            pltpu.VMEM((1024, 256), F32),
            pltpu.VMEM((1024, HD), F32),
            pltpu.VMEM((512, HD), BF16),
            pltpu.VMEM((512, HD), BF16),
            pltpu.VMEM((8, TOK), F32),
            pltpu.VMEM((8, TOK), F32),
            pltpu.VMEM((2, TOK, 512), BF16),
            pltpu.VMEM((2, 2, 512, QUARTER), BF16),
            pltpu.VMEM((TOK, QUARTER), BF16),
            pltpu.VMEM((TOK, QUARTER), BF16),
            pltpu.VMEM((2, 8, QUARTER), F32),
            pltpu.VMEM((2, TOK, QUARTER), BF16),
            pltpu.VMEM((4, 8, TOK), F32),
            pltpu.VMEM((2, TOK, 384), BF16),
            pltpu.VMEM((384, TOK), F32),
            pltpu.VMEM((2, 256, 256), BF16),
            pltpu.VMEM((384, HALF), F32),
            pltpu.VMEM((32, SLOT_ROWS, 128), BF16),
            pltpu.VMEM((2, 32, SLOT_ROWS, 128), BF16),
            pltpu.VMEM((GROUP_ROWS, D), BF16),
            pltpu.VMEM((2, D, 2 * HID), BF16),
            pltpu.VMEM((2, HID, D), BF16),
            pltpu.VMEM((GROUPS, GROUP_ROWS, HALF), BF16),
            pltpu.VMEM((GROUPS, GROUP_ROWS, HALF), BF16),
            pltpu.VMEM((GROUPS, GROUP_ROWS, HALF), F32),
            pltpu.VMEM((32, SLOT_ROWS, 128), BF16),
            pltpu.VMEM((32, SLOT_ROWS, 128), BF16),
            pltpu.VMEM((384, HALF), BF16),
            pltpu.VMEM((TOK, QUARTER), BF16),
            pltpu.VMEM((TOK, QUARTER), BF16),
            dma((32,)),
            dma((32,)),
            dma((32,)),
            dma((32,)),
            dma((GROUPS,)),
            dma((GROUPS,)),
            dma((32,)),
            dma,
            dma,
            dma,
            dma,
            dma,
            dma((11,)),
            dma((11,)),
            dma((4,)),
            dma((4,)),
            dma((4,)),
        ],
        compiler_params=pltpu.CompilerParams(
            collective_id=0,
            has_side_effects=True,
            vmem_limit_bytes=58 * 1024 * 1024,
        ),
        cost_estimate=pl.CostEstimate(
            flops=8_000_000_000, bytes_accessed=20_000_000, transcendentals=5_000_000
        ),
    )(
        queries,
        key_heads,
        value_heads,
        residual,
        out_proj,
        norm_gain.reshape(1, QUARTER),
        routes,
        combine_weight,
        gate_up.reshape(D, 2 * HID),
        down_proj.reshape(HID, D),
    )


def solution(mesh):
    placed = (
        P("seq", "head"),
        P("seq", "head"),
        P("seq", "head"),
        P("seq", "head"),
        P("head", None),
        P("head"),
        P("seq", None),
        P("seq", None),
        P("seq", None, None, "head"),
        P("seq", "head", None),
    )
    return jax.shard_map(
        body,
        mesh=mesh,
        in_specs=placed,
        out_specs=(P("seq", "head"), P("seq", "head")),
        check_vma=False,
    )
```

```python
import math

import jax
import jax.numpy as jnp
from jax import lax
from jax.experimental import pallas as pl
from jax.experimental.pallas import tpu as pltpu
from jax.sharding import PartitionSpec as P

D = 3584
HD = 128
TOK = 128
QUARTER = 896
HALF = 1792
HID = 320
ROWS_A = 80
SLOT_ROWS = 144
GROUP = 8
GROUPS = 4
GROUP_ROWS = 80
EPSILON = 1e-06
SCALE2 = math.log2(math.e) / math.sqrt(HD)
MESH = pl.DeviceIdType.MESH
F32 = jnp.float32
BF16 = jnp.bfloat16


def dot(a, b):
    return jnp.dot(a, b, preferred_element_type=F32)


def dot_nt(a, b):
    return lax.dot_general(a, b, (((1,), (1,)), ((), ())), preferred_element_type=F32)


def iota(shape, dim):
    return lax.broadcasted_iota(jnp.int32, shape, dim)


def kernel(
    q_ref,
    k_ref,
    v_ref,
    residual_ref,
    out_proj_ref,
    gain_ref,
    routes_ref,
    weight_ref,
    gate_up_ref,
    down_ref,
    mid_ref,
    out_ref,
    kv,
    qr,
    acc,
    row_max,
    row_sum,
    part_send,
    part_recv,
    stat_send,
    stat_recv,
    att,
    wo,
    rs_send,
    rs_recv,
    gains,
    mid_half,
    squares,
    wc,
    onehot,
    perm,
    ymat,
    send_buf,
    xbuf,
    xmat,
    gu,
    wd,
    po_send,
    po_recv,
    po_own,
    ret_send,
    ret,
    rmat,
    comb_send,
    comb_recv,
    ra,
    rb,
    rd,
    rp,
    rpo,
    spo,
    rr,
    sa,
    sb,
    sd,
    sp,
    sr,
    misc_send,
    misc_recv,
    weight_send,
    weight_recv,
    weight_local,
    column,
):
    seq, head = lax.axis_index("seq"), lax.axis_index("head")
    y, z = lax.div(seq, 16), lax.rem(seq, 8)
    xh = lax.rem(lax.div(seq, 8), 2)
    xl, core = lax.div(head, 2), lax.rem(head, 2)
    other = 1 - core
    z_even, y_even, core_zero = lax.rem(z, 2) == 0, lax.rem(y, 2) == 0, core == 0
    my_kv = z * 4 + y
    my_j = y * 8 + z
    far_h, far_l = (xh + core) % 2, (xl + core) % 2
    half_in = far_l

    def dev(y_, xh_, z_, xl_, core_):
        return {"seq": (y_ * 2 + xh_) * 8 + z_, "head": xl_ * 2 + core_}

    partner = dev(y, xh, z, xl, other)
    pair = dev(y, xh, z, 1 - xl, core)
    diagonal = dev(y, xh, z, 1 - xl, other)
    twin = dev(y, 1 - xh, z, xl, core)
    cross = dev(y, 1 - xh, z, 1 - xl, core)

    def wrap(a, n):
        return lax.rem(a + n, n)

    yp, ym, y2 = wrap(y + 1, 4), wrap(y - 1, 4), wrap(y + 2, 4)
    zp, zm = wrap(z + 1, 8), wrap(z - 1, 8)

    def far(j):
        return dev(lax.div(j, 8), far_h, lax.rem(j, 8), far_l, core)

    barrier = pltpu.get_barrier_semaphore()

    def greet(device):
        pl.semaphore_signal(barrier, inc=1, device_id=device, device_id_type=MESH)

    for device in (
        dev(yp, xh, z, xl, core),
        dev(ym, xh, z, xl, core),
        dev(y, xh, zp, xl, core),
        dev(y, xh, zm, xl, core),
        twin,
        partner,
        pair,
        diagonal,
        cross,
    ):
        greet(device)

    for j in range(4):
        qr[j * TOK : (j + 1) * TOK, :] = q_ref[:, j * HD : (j + 1) * HD]
    kv[my_kv, :, 0:128] = k_ref[...]
    kv[my_kv, :, 128:256] = v_ref[...]
    gains[core, :, :] = jnp.broadcast_to(gain_ref[...].astype(F32).reshape(1, QUARTER), (8, QUARTER))
    pl.semaphore_wait(barrier, 9)

    def rcopy(src, dst, send, recv, device):
        return pltpu.make_async_remote_copy(
            src_ref=src,
            dst_ref=dst,
            send_sem=send,
            recv_sem=recv,
            device_id=device,
            device_id_type=MESH,
        )

    def part_a(b):
        return kv.at[b, pl.ds(0, ROWS_A)]

    def part_b(b):
        return kv.at[b, pl.ds(ROWS_A, TOK - ROWS_A)]

    def send_a(zb, yb, y_, z_):
        b = zb * 4 + yb
        rcopy(part_a(b), part_a(b), sa, ra.at[b], dev(y_, xh, z_, xl, core)).start()

    def send_b(zb, yb, y_, z_):
        b = zb * 4 + yb
        rcopy(part_b(b), part_b(b), sb, rb.at[b], dev(y_, xh, z_, xl, core)).start()

    def wait_a(zb, yb):
        b = zb * 4 + yb
        pltpu.make_async_copy(part_a(b), part_a(b), ra.at[b]).wait()

    def wait_b(zb, yb):
        b = zb * 4 + yb
        pltpu.make_async_copy(part_b(b), part_b(b), rb.at[b]).wait()

    send_a(z, y, y, zp)
    send_a(z, y, y, zm)
    send_b(z, y, yp, z)
    send_b(z, y, ym, z)
    send_a(z, y, yp, z)
    send_a(z, y, ym, z)
    send_b(z, y, y, zp)
    send_b(z, y, y, zm)
    q_copy = rcopy(
        qr.at[pl.ds(0, 512)], qr.at[pl.ds(512, 512)], misc_send.at[0], misc_recv.at[0], twin
    )
    q_copy.start()
    gain_copy = rcopy(gains.at[core], gains.at[core], misc_send.at[1], misc_recv.at[1], partner)
    gain_copy.start()

    wo_copies = []
    for hf in range(2):
        mine = pl.ds(pl.multiple_of((hf * 2 + core) * QUARTER, 128), QUARTER)
        theirs = pl.ds(pl.multiple_of((hf * 2 + other) * QUARTER, 128), QUARTER)
        wo_copies.append(
            rcopy(
                out_proj_ref.at[:, theirs],
                wo.at[core, hf],
                weight_send.at[hf],
                weight_recv.at[hf],
                partner,
            )
        )
        wo_copies[-1].start()
        wo_copies.append(
            pltpu.make_async_copy(out_proj_ref.at[:, mine], wo.at[core, hf], weight_local.at[hf])
        )
    for copy in wo_copies[1::2]:
        copy.start()
    ffn_copies = []
    for n, (src, dst) in enumerate(((gate_up_ref, gu), (down_ref, wd))):
        remote = rcopy(
            src, dst.at[core], weight_send.at[2 + n], weight_recv.at[2 + n], partner
        )
        local = pltpu.make_async_copy(src, dst.at[core], weight_local.at[2 + n])
        remote.start()
        local.start()
        ffn_copies += [remote, local]

    acc[...] = jnp.zeros((1024, HD), F32)
    row_sum[...] = jnp.zeros((1024, HD), F32)
    row_max[...] = jnp.full((1024, HD), -1e30, F32)

    eye = iota((TOK, TOK), 0) == iota((TOK, TOK), 1)

    def to_row(column):
        return jnp.sum(jnp.where(eye, column, 0.0), axis=0, keepdims=True)

    def to_column(row):
        return jnp.sum(jnp.where(eye, row, 0.0), axis=1, keepdims=True)

    lane = iota((1, 384), 1)
    main = lane < 256
    extra = lane - 256
    j_row = jnp.where(main, lax.shift_right_logical(lane, 3), lax.shift_right_logical(jnp.maximum(extra, 0), 1))
    s_row = jnp.where(main, lane & 7, 8 + (extra & 1))
    e_row = lax.shift_right_logical(j_row, 3) * 16 + far_h * 8 + (j_row & 7)
    e_row = jnp.where(j_row < 32, e_row, -1).astype(F32)
    named = jnp.zeros((TOK, 384), F32)
    weight = jnp.zeros((TOK, 384), F32)
    for k in range(4):
        same = to_column(routes_ref[k : k + 1, :].astype(F32)) == e_row
        named = jnp.where(same, 1.0, named)
        weight = jnp.where(same, to_column(weight_ref[k : k + 1, :]), weight)
    earlier = jnp.where(iota((TOK, TOK), 1) < iota((TOK, TOK), 0), 1.0, 0.0).astype(BF16)
    count = dot(earlier, named.astype(BF16))
    taken = jnp.where(count == s_row.astype(F32), named, 0.0)
    weight = weight * taken
    high = weight.astype(BF16)
    wc[0] = high
    wc[1] = (weight - high.astype(F32)).astype(BF16)
    onehot[...] = taken.T
    for which in range(2):
        o, i = iota((256, 256), which), iota((256, 256), 1 - which)
        rem = o & 31
        source = lax.shift_right_logical(rem, 1) * 16 + lax.shift_right_logical(o, 5) * 2 + (rem & 1)
        perm[which] = jnp.where((source == i) & (rem < 28), 1.0, 0.0).astype(BF16)
    rmat[...] = jnp.zeros((384, HALF), BF16)

    def flash(zb, first, count):
        block = kv[pl.ds(zb * 4, 4)]
        keys = block[:, :, 0:128].reshape(512, HD)
        values = block[:, :, 128:256].reshape(512, HD)

        def tile(t, carry):
            rows = pl.ds(pl.multiple_of(first + t * 256, 256), 256)
            scores = dot_nt(qr[rows, :], keys)
            old = row_max[rows, :]
            new = jnp.maximum(old, jnp.max(scores, axis=1, keepdims=True))
            p = jnp.exp2((scores - new[:, 0:1]) * SCALE2)
            fade = jnp.exp2((old - new) * SCALE2)
            lanes = (p[:, 0:128] + p[:, 128:256]) + (p[:, 256:384] + p[:, 384:512])
            row_sum[rows, :] = row_sum[rows, :] * fade + lanes
            acc[rows, :] = acc[rows, :] * fade + dot(p.astype(BF16), values)
            row_max[rows, :] = new
            return carry

        lax.fori_loop(0, count // 256, tile, 0)

    def y_stage(zb):
        even = lax.rem(zb, 2) == 0
        wait_a(zb, ym)

        @pl.when(even)
        def _():
            send_a(zb, ym, yp, z)

        wait_a(zb, yp)

        @pl.when(jnp.logical_not(even))
        def _():
            send_a(zb, yp, ym, z)

    for yb, forward, to in ((ym, z_even, yp), (yp, jnp.logical_not(z_even), ym)):
        wait_b(z, yb)
        send_b(z, yb, y, zp)
        send_b(z, yb, y, zm)

        @pl.when(forward)
        def _():
            send_b(z, yb, to, z)

    y_stage(z)
    wait_b(z, y2)
    send_b(z, y2, y, zp)
    send_b(z, y2, y, zm)

    def z_stage(d):
        for zb, to, parity in ((wrap(z - d, 8), zp, 0), (wrap(z + d, 8), zm, 1)):
            wait_a(zb, y)
            goes = (d < 3) | ((d == 3) & (lax.rem(y, 2) == parity))

            @pl.when(goes)
            def _():
                send_a(zb, y, y, to)

            send_a(zb, y, yp, z)
            send_a(zb, y, ym, z)

            def each(yb, carry):
                wait_b(zb, yb)

                @pl.when((d < 3) | ((d == 3) & (lax.rem(yb, 2) == parity)))
                def _():
                    send_b(zb, yb, y, to)

                return carry

            lax.fori_loop(0, 4, each, 0)

    def step(d, carry):
        z_stage(d)

        @pl.when(d == 1)
        def _():
            q_copy.wait_recv()
            wait_a(z, y2)
            flash(z, 0, 1024)

        @pl.when(d > 1)
        def _():
            for zb in (wrap(z - d + 1, 8), wrap(z + d - 1, 8)):
                wait_a(zb, y2)
                flash(zb, 0, 1024)

        y_stage(wrap(z - d, 8))
        y_stage(wrap(z + d, 8))
        return carry

    lax.fori_loop(1, 4, step, 0)
    zf = wrap(z + 4, 8)
    wait_a(zf, y)
    send_a(zf, y, yp, z)
    send_a(zf, y, ym, z)
    for zb in (wrap(z - 3, 8), wrap(z + 3, 8)):
        wait_a(zb, y2)
        flash(zb, 0, 1024)
    y_stage(zf)
    wait_a(zf, y2)
    for yb in range(4):
        wait_b(zf, yb)

    @pl.when(core == 1)
    def _():
        pl.semaphore_signal(column, inc=1, device_id=cross, device_id_type=MESH)

    flash(zf, 512, 512)
    for j in range(4):
        rows = pl.ds(512 + j * TOK, TOK)
        total = jnp.sum(row_sum[rows, :], axis=1, keepdims=True)
        part_send[j * TOK : (j + 1) * TOK, :] = (acc[rows, :] / total).astype(BF16)
        stat_send[j : j + 1, :] = to_row(row_max[rows, :] * SCALE2 + jnp.log2(total))
    stat_send[4:8, :] = jnp.zeros((4, TOK), F32)
    part_copy = rcopy(part_send, part_recv, misc_send.at[2], misc_recv.at[2], twin)
    stat_copy = rcopy(stat_send, stat_recv, misc_send.at[3], misc_recv.at[3], twin)
    part_copy.start()
    stat_copy.start()
    flash(zf, 0, 512)
    part_copy.wait_recv()
    stat_copy.wait_recv()
    for j in range(4):
        rows = slice(j * TOK, (j + 1) * TOK)
        total = jnp.sum(row_sum[rows, :], axis=1, keepdims=True)
        own = acc[rows, :] / total
        own_stat = row_max[rows, :] * SCALE2 + jnp.log2(total)
        their_stat = to_column(stat_recv[j : j + 1, :])
        own_share = 1.0 / (1.0 + jnp.exp2(their_stat - own_stat))
        their_share = 1.0 / (1.0 + jnp.exp2(own_stat - their_stat))
        att[core, :, rows] = (
            own * own_share + part_recv[rows, :].astype(F32) * their_share
        ).astype(BF16)
    att_copy = rcopy(att.at[core], att.at[core], misc_send.at[4], misc_recv.at[4], partner)
    att_copy.start()
    for copy in wo_copies[0::2]:
        copy.wait_recv()
    for copy in wo_copies[1::2]:
        copy.wait()
    gain_copy.wait_recv()
    att_copy.wait_recv()

    def project(hf):
        return dot(att[0], wo[0, hf]) + dot(att[1], wo[1, hf])

    rs_send[...] = project(1 - xl).astype(BF16)
    rs_copy = rcopy(rs_send, rs_recv, misc_send.at[5], misc_recv.at[5], pair)
    rs_copy.start()
    own = project(xl) + residual_ref[...].astype(F32)
    rs_copy.wait_recv()
    middle = (own + rs_recv[...].astype(F32)).astype(BF16)
    mid_half[core, :, :] = middle
    mid_copy = rcopy(
        mid_half.at[core], mid_half.at[core], misc_send.at[6], misc_recv.at[6], partner
    )
    mid_copy.start()
    mid_ref[...] = middle
    mid_float = middle.astype(F32)
    squares[head] = jnp.broadcast_to(
        to_row(jnp.sum(mid_float * mid_float, axis=1, keepdims=True)), (8, TOK)
    )
    square_copies = [
        rcopy(squares.at[head], squares.at[head], misc_send.at[7 + n], misc_recv.at[7 + n], device)
        for n, device in enumerate((partner, pair, diagonal))
    ]
    for copy in square_copies:
        copy.start()
    mid_copy.wait_recv()
    hot = onehot[...]
    hot16 = hot.astype(BF16)
    for c in range(2):
        ymat[:, c * QUARTER : (c + 1) * QUARTER] = dot(hot16, mid_half[c])
    for copy in square_copies:
        copy.wait_recv()
    total = squares[0, 0:1] + squares[1, 0:1] + squares[2, 0:1] + squares[3, 0:1]
    inverse = lax.rsqrt(total / D + EPSILON)
    row_scale = jnp.sum(hot * inverse, axis=1, keepdims=True)

    def lane_block(c):
        return slice(c * 128, (c + 1) * 128)

    def scaled(rows, c):
        q, inner = c // 7, c % 7
        return ymat[rows, lane_block(c)] * row_scale[rows] * gains[q, 0:1, lane_block(inner)]

    for c in range(0, 14, 2):
        both = [scaled(slice(0, 256), c + n).reshape(32, 8, 128) for n in range(2)]
        send_buf[:, c * 8 : c * 8 + 16, :] = jnp.concatenate(both, axis=1).astype(BF16)
    for g in range(4):
        rows = slice(256 + 16 * g, 272 + 16 * g)
        stack = jnp.concatenate(
            [scaled(rows, c).astype(BF16) for c in range(14)] + [jnp.zeros((32, 128), BF16)], axis=0
        )
        send_buf[8 * g : 8 * g + 8, 112:144, :] = (
            dot(perm[0], stack).reshape(8, 32, 128).astype(BF16)
        )

    def exchange(buffer, place, send, recv, first, count):
        def one(i, carry):
            j = lax.rem(my_j + i, 32)
            rcopy(buffer.at[j], place(), send, recv.at[my_j], far(j)).start()
            return carry

        lax.fori_loop(first, count, one, 0)

    def landing():
        return xbuf.at[xl, my_j]

    @pl.when(core == 1)
    def _():
        pl.semaphore_wait(column, 1)

    @pl.when(core_zero)
    def _():
        pltpu.make_async_copy(send_buf.at[my_j], xbuf.at[xl, my_j], rd.at[my_j]).start()

    @pl.when(core == 1)
    def _():
        rcopy(send_buf.at[my_j], landing(), sd, rd.at[my_j], far(my_j)).start()

    exchange(send_buf, landing, sd, rd, 1, 32)

    for copy in ffn_copies[0::2]:
        copy.wait_recv()
    for copy in ffn_copies[1::2]:
        copy.wait()

    def source(i):
        return wrap(my_j - i, 32)

    def forward(g):
        def one(n, carry):
            s = source(g * GROUP + n)
            block = xbuf.at[half_in, s]
            pltpu.make_async_copy(block, block, rd.at[s]).wait()
            rcopy(block, block, sp, rp.at[s], pair).start()
            return carry

        lax.fori_loop(0, GROUP, one, 0)

    def gather_rows(g):
        def await_pair(n, carry):
            s = source(g * GROUP + n)
            block = xbuf.at[1 - half_in, s]
            pltpu.make_async_copy(block, block, rp.at[s]).wait()
            return carry

        lax.fori_loop(0, GROUP, await_pair, 0)
        for half in range(2):
            for p in range(GROUP // 2):
                both = [
                    xbuf[half, source(g * GROUP + 2 * p + n), 0:112, :]
                    .astype(F32)
                    .reshape(14, 8, 128)
                    for n in range(2)
                ]
                rows = jnp.concatenate(both, axis=1).astype(BF16)
                for c in range(14):
                    xmat[16 * p : 16 * p + 16, lane_block(half * 14 + c)] = rows[c]
            stack = jnp.concatenate(
                [xbuf[half, source(g * GROUP + n), 112:144, :] for n in range(GROUP)], axis=0
            )
            rows = dot(perm[1], stack).astype(BF16)
            for c in range(14):
                xmat[64:80, lane_block(half * 14 + c)] = rows[16 * c : 16 * c + 16]

    def experts(g):
        x = xmat[...]
        parts = []
        for c in range(2):
            gate, up = dot_nt(x, gu[c, 0:HID]), dot_nt(x, gu[c, HID : 2 * HID])
            parts.append((gate / (1.0 + jnp.exp(-gate)) * up).astype(BF16))

        def result(half, n):
            columns = pl.ds(pl.multiple_of(half * HALF + n * QUARTER, 128), QUARTER)
            return dot(parts[0], wd[0, :, columns]) + dot(parts[1], wd[1, :, columns])

        for n in range(2):
            po_send[g, :, n * QUARTER : (n + 1) * QUARTER] = result(1 - half_in, n).astype(BF16)
        rcopy(po_send.at[g], po_recv.at[g], spo.at[g], rpo.at[g], pair).start()
        for n in range(2):
            po_own[g, :, n * QUARTER : (n + 1) * QUARTER] = result(half_in, n)

    def give_back(g):
        pltpu.make_async_copy(po_recv.at[g], po_recv.at[g], rpo.at[g]).wait()
        first = pl.multiple_of(g * GROUP, GROUP)

        def summed(rows, c):
            return po_own[g, rows, lane_block(c)] + po_recv[g, rows, lane_block(c)].astype(F32)

        for c in range(0, 14, 2):
            both = [summed(slice(0, 64), c + n).reshape(8, 8, 128) for n in range(2)]
            ret_send[pl.ds(first, 8), c * 8 : c * 8 + 16, :] = jnp.concatenate(both, axis=1).astype(
                BF16
            )
        stack = jnp.concatenate(
            [summed(slice(64, 80), c).astype(BF16) for c in range(14)]
            + [jnp.zeros((32, 128), BF16)],
            axis=0,
        )
        ret_send[pl.ds(first, 8), 112:144, :] = dot(perm[0], stack).reshape(8, 32, 128).astype(BF16)

        def one(n, carry):
            i = g * GROUP + n
            s = source(i)

            @pl.when(core_zero & (i == 0))
            def _():
                pltpu.make_async_copy(ret_send.at[i], ret.at[my_j], rr.at[my_j]).start()

            @pl.when(jnp.logical_not(core_zero & (i == 0)))
            def _():
                rcopy(ret_send.at[i], ret.at[my_j], sr, rr.at[my_j], far(s)).start()

            return carry

        lax.fori_loop(0, GROUP, one, 0)

    forward(0)

    def turn(g, carry):
        @pl.when(g < GROUPS - 1)
        def _():
            forward(g + 1)

        gather_rows(g)
        experts(g)

        @pl.when(g > 0)
        def _():
            give_back(g - 1)

        return carry

    lax.fori_loop(0, GROUPS, turn, 0)
    give_back(GROUPS - 1)

    def await_return(i, carry):
        j = lax.rem(my_j + i, 32)
        pltpu.make_async_copy(ret.at[j], ret.at[j], rr.at[j]).wait()
        return carry

    lax.fori_loop(0, 32, await_return, 0)
    for c in range(0, 14, 2):
        both = ret[:, c * 8 : c * 8 + 16, :].astype(F32)
        for n in range(2):
            rmat[0:256, lane_block(c + n)] = both[:, 8 * n : 8 * n + 8].reshape(256, 128).astype(BF16)
    for g in range(4):
        stack = ret[8 * g : 8 * g + 8, 112:144, :].reshape(256, 128)
        rows = dot(perm[1], stack).astype(BF16)
        for c in range(14):
            rmat[256 + 16 * g : 272 + 16 * g, lane_block(c)] = rows[16 * c : 16 * c + 16]

    def combined(which):
        columns = pl.ds(pl.multiple_of(which * QUARTER, 128), QUARTER)
        rows = rmat[:, columns]
        return dot(wc[0], rows) + dot(wc[1], rows)

    comb_send[...] = combined(other).astype(BF16)
    comb_copy = rcopy(comb_send, comb_recv, misc_send.at[10], misc_recv.at[10], partner)
    comb_copy.start()
    own = combined(core)
    comb_copy.wait_recv()
    out_ref[...] = (own + comb_recv[...].astype(F32)).astype(BF16)

    for copy in (
        [q_copy, gain_copy, part_copy, stat_copy, att_copy, rs_copy, mid_copy, comb_copy]
        + square_copies
        + wo_copies[0::2]
        + ffn_copies[0::2]
    ):
        copy.wait_send()
    for g in range(GROUPS):
        pltpu.make_async_copy(po_send.at[g], po_send.at[g], spo.at[g]).wait()

    def drain(ref, sem):
        pltpu.make_async_copy(ref, ref, sem).wait()

    drain(kv.at[pl.ds(0, 31), pl.ds(0, ROWS_A)], sa)
    drain(kv.at[pl.ds(0, 31), pl.ds(ROWS_A, TOK - ROWS_A)], sb)
    drain(xbuf.at[0], sp)
    for sem in (sd, sr):

        @pl.when(core_zero)
        def _():
            drain(send_buf.at[pl.ds(0, 31)], sem)

        @pl.when(core == 1)
        def _():
            drain(send_buf, sem)


def body(
    queries,
    key_heads,
    value_heads,
    residual,
    out_proj,
    norm_gain,
    routes,
    combine_weight,
    gate_up,
    down_proj,
):
    vmem = pl.BlockSpec(memory_space=pltpu.VMEM)
    hbm = pl.BlockSpec(memory_space=pl.ANY)
    dma = pltpu.SemaphoreType.DMA
    return pl.pallas_call(
        kernel,
        out_shape=(
            jax.ShapeDtypeStruct((TOK, QUARTER), BF16),
            jax.ShapeDtypeStruct((TOK, QUARTER), BF16),
        ),
        in_specs=[vmem, vmem, vmem, vmem, hbm, vmem, vmem, vmem, hbm, hbm],
        out_specs=(vmem, vmem),
        scratch_shapes=[
            pltpu.VMEM((32, TOK, 256), BF16),
            pltpu.VMEM((1024, HD), BF16),
            pltpu.VMEM((1024, HD), F32),
            pltpu.VMEM((1024, HD), F32),
            pltpu.VMEM((1024, HD), F32),
            pltpu.VMEM((512, HD), BF16),
            pltpu.VMEM((512, HD), BF16),
            pltpu.VMEM((8, TOK), F32),
            pltpu.VMEM((8, TOK), F32),
            pltpu.VMEM((2, TOK, 512), BF16),
            pltpu.VMEM((2, 2, 512, QUARTER), BF16),
            pltpu.VMEM((TOK, QUARTER), BF16),
            pltpu.VMEM((TOK, QUARTER), BF16),
            pltpu.VMEM((2, 8, QUARTER), F32),
            pltpu.VMEM((2, TOK, QUARTER), BF16),
            pltpu.VMEM((4, 8, TOK), F32),
            pltpu.VMEM((2, TOK, 384), BF16),
            pltpu.VMEM((384, TOK), F32),
            pltpu.VMEM((2, 256, 256), BF16),
            pltpu.VMEM((384, HALF), F32),
            pltpu.VMEM((32, SLOT_ROWS, 128), BF16),
            pltpu.VMEM((2, 32, SLOT_ROWS, 128), BF16),
            pltpu.VMEM((GROUP_ROWS, D), BF16),
            pltpu.VMEM((2, 2 * HID, D), BF16),
            pltpu.VMEM((2, HID, D), BF16),
            pltpu.VMEM((GROUPS, GROUP_ROWS, HALF), BF16),
            pltpu.VMEM((GROUPS, GROUP_ROWS, HALF), BF16),
            pltpu.VMEM((GROUPS, GROUP_ROWS, HALF), F32),
            pltpu.VMEM((32, SLOT_ROWS, 128), BF16),
            pltpu.VMEM((32, SLOT_ROWS, 128), BF16),
            pltpu.VMEM((384, HALF), BF16),
            pltpu.VMEM((TOK, QUARTER), BF16),
            pltpu.VMEM((TOK, QUARTER), BF16),
            dma((32,)),
            dma((32,)),
            dma((32,)),
            dma((32,)),
            dma((GROUPS,)),
            dma((GROUPS,)),
            dma((32,)),
            dma,
            dma,
            dma,
            dma,
            dma,
            dma((11,)),
            dma((11,)),
            dma((4,)),
            dma((4,)),
            dma((4,)),
            pltpu.SemaphoreType.REGULAR,
        ],
        compiler_params=pltpu.CompilerParams(
            collective_id=0,
            has_side_effects=True,
            vmem_limit_bytes=58 * 1024 * 1024,
        ),
        cost_estimate=pl.CostEstimate(
            flops=8_000_000_000, bytes_accessed=20_000_000, transcendentals=5_000_000
        ),
    )(
        queries,
        key_heads,
        value_heads,
        residual,
        out_proj,
        norm_gain,
        routes.T,
        combine_weight.T,
        gate_up.reshape(D, 2 * HID).T,
        down_proj.reshape(HID, D),
    )


def solution(mesh):
    placed = (
        P("seq", "head"),
        P("seq", "head"),
        P("seq", "head"),
        P("seq", "head"),
        P("head", None),
        P("head"),
        P("seq", None),
        P("seq", None),
        P("seq", None, None, "head"),
        P("seq", "head", None),
    )
    return jax.shard_map(
        body,
        mesh=mesh,
        in_specs=placed,
        out_specs=(P("seq", "head"), P("seq", "head")),
        check_vma=False,
    )
```

```python
import math

import jax
import jax.numpy as jnp
from jax import lax
from jax.experimental import pallas as pl
from jax.experimental.pallas import tpu as pltpu
from jax.sharding import PartitionSpec as P

D = 3584
HD = 128
TOK = 128
QUARTER = 896
HALF = 1792
HID = 320
SLOT_ROWS = 144
GROUP = 8
GROUPS = 4
GROUP_ROWS = 80
EPSILON = 1e-06
SCALE2 = math.log2(math.e) / math.sqrt(HD)
MESH = pl.DeviceIdType.MESH
F32 = jnp.float32
BF16 = jnp.bfloat16


def dot(a, b):
    return jnp.dot(a, b, preferred_element_type=F32)


def dot_nt(a, b):
    return lax.dot_general(a, b, (((1,), (1,)), ((), ())), preferred_element_type=F32)


def iota(shape, dim):
    return lax.broadcasted_iota(jnp.int32, shape, dim)


def kernel(
    q_ref,
    k_ref,
    v_ref,
    residual_ref,
    out_proj_ref,
    gain_ref,
    routes_ref,
    weight_ref,
    gate_up_ref,
    down_ref,
    mid_ref,
    out_ref,
    kv,
    qr,
    acc,
    row_max,
    row_sum,
    part_send,
    part_recv,
    stat_send,
    stat_recv,
    att,
    wo,
    rs_send,
    rs_recv,
    gains,
    mid_half,
    squares,
    wc,
    onehot,
    perm,
    ymat,
    send_buf,
    xbuf,
    xmat,
    gu,
    wd,
    po_send,
    po_recv,
    po_own,
    ret_send,
    ret,
    rmat,
    comb_send,
    comb_recv,
    ra,
    rb,
    rd,
    rp,
    rpo,
    spo,
    rr,
    sa,
    sb,
    sd,
    sp,
    sr,
    misc_send,
    misc_recv,
    weight_send,
    weight_recv,
    weight_local,
    column,
):
    seq, head = lax.axis_index("seq"), lax.axis_index("head")
    y, z = lax.div(seq, 16), lax.rem(seq, 8)
    xh = lax.rem(lax.div(seq, 8), 2)
    xl, core = lax.div(head, 2), lax.rem(head, 2)
    other = 1 - core
    core_zero = core == 0
    my_kv = z * 4 + y
    my_j = y * 8 + z
    far_h, far_l = (xh + core) % 2, (xl + core) % 2
    half_in = far_l

    def dev(y_, xh_, z_, xl_, core_):
        return {"seq": (y_ * 2 + xh_) * 8 + z_, "head": xl_ * 2 + core_}

    partner = dev(y, xh, z, xl, other)
    pair = dev(y, xh, z, 1 - xl, core)
    diagonal = dev(y, xh, z, 1 - xl, other)
    twin = dev(y, 1 - xh, z, xl, core)
    cross = dev(y, 1 - xh, z, 1 - xl, core)

    def wrap(a, n):
        return lax.rem(a + n, n)

    yp, ym, y2 = wrap(y + 1, 4), wrap(y - 1, 4), wrap(y + 2, 4)
    zp, zm = wrap(z + 1, 8), wrap(z - 1, 8)

    def far(j):
        return dev(lax.div(j, 8), far_h, lax.rem(j, 8), far_l, core)

    barrier = pltpu.get_barrier_semaphore()

    def greet(device):
        pl.semaphore_signal(barrier, inc=1, device_id=device, device_id_type=MESH)

    for device in (
        dev(yp, xh, z, xl, core),
        dev(ym, xh, z, xl, core),
        dev(y2, xh, z, xl, core),
        dev(y, xh, zp, xl, core),
        dev(y, xh, zm, xl, core),
        twin,
        partner,
        pair,
        diagonal,
        cross,
    ):
        greet(device)

    for j in range(4):
        qr[j * TOK : (j + 1) * TOK, :] = q_ref[:, j * HD : (j + 1) * HD]
    kv[my_kv, :, 0:128] = k_ref[...]
    kv[my_kv, :, 128:256] = v_ref[...]
    gains[core, :, :] = jnp.broadcast_to(gain_ref[...].astype(F32).reshape(1, QUARTER), (8, QUARTER))
    pl.semaphore_wait(barrier, 10)

    def rcopy(src, dst, send, recv, device):
        return pltpu.make_async_remote_copy(
            src_ref=src,
            dst_ref=dst,
            send_sem=send,
            recv_sem=recv,
            device_id=device,
            device_id_type=MESH,
        )

    def y_block(yb):
        return kv.at[z * 4 + yb]

    def bundle(zb, h):
        return kv.at[pl.ds(zb * 4 + h * 2, 2)]

    def send_bundle(zb, h, to):
        part = bundle(zb, h)
        rcopy(part, part, sa, ra.at[zb * 2 + h], dev(y, xh, to, xl, core)).start()

    def wait_bundle(zb, h):
        part = bundle(zb, h)
        pltpu.make_async_copy(part, part, ra.at[zb * 2 + h]).wait()

    near = y + 1 - 2 * lax.rem(y, 2)
    others = (near, lax.rem(near + 2, 4), y2)
    for yb in others:
        rcopy(y_block(y), y_block(y), sb, rb.at[y], dev(yb, xh, z, xl, core)).start()
    q_copy = rcopy(
        qr.at[pl.ds(0, 512)], qr.at[pl.ds(512, 512)], misc_send.at[0], misc_recv.at[0], twin
    )
    q_copy.start()
    gain_copy = rcopy(gains.at[core], gains.at[core], misc_send.at[1], misc_recv.at[1], partner)
    gain_copy.start()

    h_near = lax.div(y, 2)
    for h, sources in ((h_near, others[0:1]), (1 - h_near, others[1:3])):
        for yb in sources:
            pltpu.make_async_copy(y_block(yb), y_block(yb), rb.at[yb]).wait()
        send_bundle(z, h, zp)
        send_bundle(z, h, zm)

    wo_copies = []
    for hf in range(2):
        mine = pl.ds(pl.multiple_of((hf * 2 + core) * QUARTER, 128), QUARTER)
        theirs = pl.ds(pl.multiple_of((hf * 2 + other) * QUARTER, 128), QUARTER)
        wo_copies.append(
            rcopy(
                out_proj_ref.at[:, theirs],
                wo.at[core, hf],
                weight_send.at[hf],
                weight_recv.at[hf],
                partner,
            )
        )
        wo_copies[-1].start()
        wo_copies.append(
            pltpu.make_async_copy(out_proj_ref.at[:, mine], wo.at[core, hf], weight_local.at[hf])
        )
    for copy in wo_copies[1::2]:
        copy.start()
    ffn_copies = []
    for n, (src, dst) in enumerate(((gate_up_ref, gu), (down_ref, wd))):
        remote = rcopy(
            src, dst.at[core], weight_send.at[2 + n], weight_recv.at[2 + n], partner
        )
        local = pltpu.make_async_copy(src, dst.at[core], weight_local.at[2 + n])
        remote.start()
        local.start()
        ffn_copies += [remote, local]

    acc[...] = jnp.zeros((1024, HD), F32)
    row_sum[...] = jnp.zeros((1024, HD), F32)
    row_max[...] = jnp.full((1024, HD), -1e30, F32)

    eye = iota((TOK, TOK), 0) == iota((TOK, TOK), 1)

    def to_row(column):
        return jnp.sum(jnp.where(eye, column, 0.0), axis=0, keepdims=True)

    def to_column(row):
        return jnp.sum(jnp.where(eye, row, 0.0), axis=1, keepdims=True)

    lane = iota((1, 384), 1)
    main = lane < 256
    extra = lane - 256
    j_row = jnp.where(main, lax.shift_right_logical(lane, 3), lax.shift_right_logical(jnp.maximum(extra, 0), 1))
    s_row = jnp.where(main, lane & 7, 8 + (extra & 1))
    e_row = lax.shift_right_logical(j_row, 3) * 16 + far_h * 8 + (j_row & 7)
    e_row = jnp.where(j_row < 32, e_row, -1).astype(F32)
    named = jnp.zeros((TOK, 384), F32)
    weight = jnp.zeros((TOK, 384), F32)
    for k in range(4):
        same = to_column(routes_ref[k : k + 1, :].astype(F32)) == e_row
        named = jnp.where(same, 1.0, named)
        weight = jnp.where(same, to_column(weight_ref[k : k + 1, :]), weight)
    earlier = jnp.where(iota((TOK, TOK), 1) < iota((TOK, TOK), 0), 1.0, 0.0).astype(BF16)
    count = dot(earlier, named.astype(BF16))
    taken = jnp.where(count == s_row.astype(F32), named, 0.0)
    weight = weight * taken
    high = weight.astype(BF16)
    wc[0] = high
    wc[1] = (weight - high.astype(F32)).astype(BF16)
    onehot[...] = taken.T
    for which in range(2):
        o, i = iota((256, 256), which), iota((256, 256), 1 - which)
        rem = o & 31
        source = lax.shift_right_logical(rem, 1) * 16 + lax.shift_right_logical(o, 5) * 2 + (rem & 1)
        perm[which] = jnp.where((source == i) & (rem < 28), 1.0, 0.0).astype(BF16)
    rmat[...] = jnp.zeros((384, HALF), BF16)

    def flash(zb, first, count):
        block = kv[pl.ds(zb * 4, 4)]
        keys = block[:, :, 0:128].reshape(512, HD)
        values = block[:, :, 128:256].reshape(512, HD)

        def tile(t, carry):
            rows = pl.ds(pl.multiple_of(first + t * 256, 256), 256)
            scores = dot_nt(qr[rows, :], keys)
            old = row_max[rows, :]
            new = jnp.maximum(old, jnp.max(scores, axis=1, keepdims=True))
            p = jnp.exp2((scores - new[:, 0:1]) * SCALE2)
            fade = jnp.exp2((old - new) * SCALE2)
            lanes = (p[:, 0:128] + p[:, 128:256]) + (p[:, 256:384] + p[:, 384:512])
            row_sum[rows, :] = row_sum[rows, :] * fade + lanes
            acc[rows, :] = acc[rows, :] * fade + dot(p.astype(BF16), values)
            row_max[rows, :] = new
            return carry

        lax.fori_loop(0, count // 256, tile, 0)

    def step(d, carry):
        ahead, behind = wrap(z - d, 8), wrap(z + d, 8)
        for h in (h_near, 1 - h_near):
            wait_bundle(ahead, h)

            @pl.when((d < 3) | (h == 0))
            def _():
                send_bundle(ahead, h, zp)

            wait_bundle(behind, h)

            @pl.when((d < 3) | (h == 1))
            def _():
                send_bundle(behind, h, zm)

        flash(ahead, 0, 1024)
        flash(behind, 0, 1024)
        return carry

    q_copy.wait_recv()
    flash(z, 0, 1024)
    lax.fori_loop(1, 4, step, 0)
    zf = wrap(z + 4, 8)
    for h in range(2):
        wait_bundle(zf, h)

    @pl.when(core == 1)
    def _():
        pl.semaphore_signal(column, inc=1, device_id=cross, device_id_type=MESH)

    flash(zf, 512, 512)
    for j in range(4):
        rows = pl.ds(512 + j * TOK, TOK)
        total = jnp.sum(row_sum[rows, :], axis=1, keepdims=True)
        part_send[j * TOK : (j + 1) * TOK, :] = (acc[rows, :] / total).astype(BF16)
        stat_send[j : j + 1, :] = to_row(row_max[rows, :] * SCALE2 + jnp.log2(total))
    stat_send[4:8, :] = jnp.zeros((4, TOK), F32)
    part_copy = rcopy(part_send, part_recv, misc_send.at[2], misc_recv.at[2], twin)
    stat_copy = rcopy(stat_send, stat_recv, misc_send.at[3], misc_recv.at[3], twin)
    part_copy.start()
    stat_copy.start()
    flash(zf, 0, 512)
    part_copy.wait_recv()
    stat_copy.wait_recv()
    for j in range(4):
        rows = slice(j * TOK, (j + 1) * TOK)
        total = jnp.sum(row_sum[rows, :], axis=1, keepdims=True)
        own = acc[rows, :] / total
        own_stat = row_max[rows, :] * SCALE2 + jnp.log2(total)
        their_stat = to_column(stat_recv[j : j + 1, :])
        own_share = 1.0 / (1.0 + jnp.exp2(their_stat - own_stat))
        their_share = 1.0 / (1.0 + jnp.exp2(own_stat - their_stat))
        att[core, :, rows] = (
            own * own_share + part_recv[rows, :].astype(F32) * their_share
        ).astype(BF16)
    att_copy = rcopy(att.at[core], att.at[core], misc_send.at[4], misc_recv.at[4], partner)
    att_copy.start()
    for copy in wo_copies[0::2]:
        copy.wait_recv()
    for copy in wo_copies[1::2]:
        copy.wait()
    gain_copy.wait_recv()
    att_copy.wait_recv()

    def project(hf):
        return dot(att[0], wo[0, hf]) + dot(att[1], wo[1, hf])

    rs_send[...] = project(1 - xl).astype(BF16)
    rs_copy = rcopy(rs_send, rs_recv, misc_send.at[5], misc_recv.at[5], pair)
    rs_copy.start()
    own = project(xl) + residual_ref[...].astype(F32)
    rs_copy.wait_recv()
    middle = (own + rs_recv[...].astype(F32)).astype(BF16)
    mid_half[core, :, :] = middle
    mid_copy = rcopy(
        mid_half.at[core], mid_half.at[core], misc_send.at[6], misc_recv.at[6], partner
    )
    mid_copy.start()
    mid_ref[...] = middle
    mid_float = middle.astype(F32)
    squares[head] = jnp.broadcast_to(
        to_row(jnp.sum(mid_float * mid_float, axis=1, keepdims=True)), (8, TOK)
    )
    square_copies = [
        rcopy(squares.at[head], squares.at[head], misc_send.at[7 + n], misc_recv.at[7 + n], device)
        for n, device in enumerate((partner, pair, diagonal))
    ]
    for copy in square_copies:
        copy.start()
    mid_copy.wait_recv()
    hot = onehot[...]
    hot16 = hot.astype(BF16)
    for c in range(2):
        ymat[:, c * QUARTER : (c + 1) * QUARTER] = dot(hot16, mid_half[c])
    for copy in square_copies:
        copy.wait_recv()
    total = squares[0, 0:1] + squares[1, 0:1] + squares[2, 0:1] + squares[3, 0:1]
    inverse = lax.rsqrt(total / D + EPSILON)
    row_scale = jnp.sum(hot * inverse, axis=1, keepdims=True)

    def lane_block(c):
        return slice(c * 128, (c + 1) * 128)

    def scaled(rows, c):
        q, inner = c // 7, c % 7
        return ymat[rows, lane_block(c)] * row_scale[rows] * gains[q, 0:1, lane_block(inner)]

    for c in range(0, 14, 2):
        both = [scaled(slice(0, 256), c + n).reshape(32, 8, 128) for n in range(2)]
        send_buf[:, c * 8 : c * 8 + 16, :] = jnp.concatenate(both, axis=1).astype(BF16)
    for g in range(4):
        rows = slice(256 + 16 * g, 272 + 16 * g)
        stack = jnp.concatenate(
            [scaled(rows, c).astype(BF16) for c in range(14)] + [jnp.zeros((32, 128), BF16)], axis=0
        )
        send_buf[8 * g : 8 * g + 8, 112:144, :] = (
            dot(perm[0], stack).reshape(8, 32, 128).astype(BF16)
        )

    def exchange(buffer, place, send, recv, first, count):
        def one(i, carry):
            j = lax.rem(my_j + i, 32)
            rcopy(buffer.at[j], place(), send, recv.at[my_j], far(j)).start()
            return carry

        lax.fori_loop(first, count, one, 0)

    def landing():
        return xbuf.at[xl, my_j]

    @pl.when(core == 1)
    def _():
        pl.semaphore_wait(column, 1)

    @pl.when(core_zero)
    def _():
        pltpu.make_async_copy(send_buf.at[my_j], xbuf.at[xl, my_j], rd.at[my_j]).start()

    @pl.when(core == 1)
    def _():
        rcopy(send_buf.at[my_j], landing(), sd, rd.at[my_j], far(my_j)).start()

    exchange(send_buf, landing, sd, rd, 1, 32)

    for copy in ffn_copies[0::2]:
        copy.wait_recv()
    for copy in ffn_copies[1::2]:
        copy.wait()

    def source(i):
        return wrap(my_j - i, 32)

    def forward(g):
        def one(n, carry):
            s = source(g * GROUP + n)
            block = xbuf.at[half_in, s]
            pltpu.make_async_copy(block, block, rd.at[s]).wait()
            rcopy(block, block, sp, rp.at[s], pair).start()
            return carry

        lax.fori_loop(0, GROUP, one, 0)

    def gather_rows(g):
        def await_pair(n, carry):
            s = source(g * GROUP + n)
            block = xbuf.at[1 - half_in, s]
            pltpu.make_async_copy(block, block, rp.at[s]).wait()
            return carry

        lax.fori_loop(0, GROUP, await_pair, 0)
        for half in range(2):
            for p in range(GROUP // 2):
                both = [
                    xbuf[half, source(g * GROUP + 2 * p + n), 0:112, :]
                    .astype(F32)
                    .reshape(14, 8, 128)
                    for n in range(2)
                ]
                rows = jnp.concatenate(both, axis=1).astype(BF16)
                for c in range(14):
                    xmat[16 * p : 16 * p + 16, lane_block(half * 14 + c)] = rows[c]
            stack = jnp.concatenate(
                [xbuf[half, source(g * GROUP + n), 112:144, :] for n in range(GROUP)], axis=0
            )
            rows = dot(perm[1], stack).astype(BF16)
            for c in range(14):
                xmat[64:80, lane_block(half * 14 + c)] = rows[16 * c : 16 * c + 16]

    def experts(g):
        x = xmat[...]
        parts = []
        for c in range(2):
            gate, up = dot_nt(x, gu[c, 0:HID]), dot_nt(x, gu[c, HID : 2 * HID])
            parts.append((gate / (1.0 + jnp.exp(-gate)) * up).astype(BF16))

        def result(half, n):
            columns = pl.ds(pl.multiple_of(half * HALF + n * QUARTER, 128), QUARTER)
            return dot(parts[0], wd[0, :, columns]) + dot(parts[1], wd[1, :, columns])

        for n in range(2):
            po_send[g, :, n * QUARTER : (n + 1) * QUARTER] = result(1 - half_in, n).astype(BF16)
        rcopy(po_send.at[g], po_recv.at[g], spo.at[g], rpo.at[g], pair).start()
        for n in range(2):
            po_own[g, :, n * QUARTER : (n + 1) * QUARTER] = result(half_in, n)

    def give_back(g):
        pltpu.make_async_copy(po_recv.at[g], po_recv.at[g], rpo.at[g]).wait()
        first = pl.multiple_of(g * GROUP, GROUP)

        def summed(rows, c):
            return po_own[g, rows, lane_block(c)] + po_recv[g, rows, lane_block(c)].astype(F32)

        for c in range(0, 14, 2):
            both = [summed(slice(0, 64), c + n).reshape(8, 8, 128) for n in range(2)]
            ret_send[pl.ds(first, 8), c * 8 : c * 8 + 16, :] = jnp.concatenate(both, axis=1).astype(
                BF16
            )
        stack = jnp.concatenate(
            [summed(slice(64, 80), c).astype(BF16) for c in range(14)]
            + [jnp.zeros((32, 128), BF16)],
            axis=0,
        )
        ret_send[pl.ds(first, 8), 112:144, :] = dot(perm[0], stack).reshape(8, 32, 128).astype(BF16)

        def one(n, carry):
            i = g * GROUP + n
            s = source(i)

            @pl.when(core_zero & (i == 0))
            def _():
                pltpu.make_async_copy(ret_send.at[i], ret.at[my_j], rr.at[my_j]).start()

            @pl.when(jnp.logical_not(core_zero & (i == 0)))
            def _():
                rcopy(ret_send.at[i], ret.at[my_j], sr, rr.at[my_j], far(s)).start()

            return carry

        lax.fori_loop(0, GROUP, one, 0)

    forward(0)

    def turn(g, carry):
        @pl.when(g < GROUPS - 1)
        def _():
            forward(g + 1)

        gather_rows(g)
        experts(g)

        @pl.when(g > 0)
        def _():
            give_back(g - 1)

        return carry

    lax.fori_loop(0, GROUPS, turn, 0)
    give_back(GROUPS - 1)

    def await_return(i, carry):
        j = lax.rem(my_j + i, 32)
        pltpu.make_async_copy(ret.at[j], ret.at[j], rr.at[j]).wait()
        return carry

    lax.fori_loop(0, 32, await_return, 0)
    for c in range(0, 14, 2):
        both = ret[:, c * 8 : c * 8 + 16, :].astype(F32)
        for n in range(2):
            rmat[0:256, lane_block(c + n)] = both[:, 8 * n : 8 * n + 8].reshape(256, 128).astype(BF16)
    for g in range(4):
        stack = ret[8 * g : 8 * g + 8, 112:144, :].reshape(256, 128)
        rows = dot(perm[1], stack).astype(BF16)
        for c in range(14):
            rmat[256 + 16 * g : 272 + 16 * g, lane_block(c)] = rows[16 * c : 16 * c + 16]

    def combined(which):
        columns = pl.ds(pl.multiple_of(which * QUARTER, 128), QUARTER)
        rows = rmat[:, columns]
        return dot(wc[0], rows) + dot(wc[1], rows)

    comb_send[...] = combined(other).astype(BF16)
    comb_copy = rcopy(comb_send, comb_recv, misc_send.at[10], misc_recv.at[10], partner)
    comb_copy.start()
    own = combined(core)
    comb_copy.wait_recv()
    out_ref[...] = (own + comb_recv[...].astype(F32)).astype(BF16)

    for copy in (
        [q_copy, gain_copy, part_copy, stat_copy, att_copy, rs_copy, mid_copy, comb_copy]
        + square_copies
        + wo_copies[0::2]
        + ffn_copies[0::2]
    ):
        copy.wait_send()
    for g in range(GROUPS):
        pltpu.make_async_copy(po_send.at[g], po_send.at[g], spo.at[g]).wait()

    def drain(ref, sem):
        pltpu.make_async_copy(ref, ref, sem).wait()

    drain(kv.at[pl.ds(0, 28)], sa)
    drain(kv.at[pl.ds(0, 3)], sb)
    drain(xbuf.at[0], sp)
    for sem in (sd, sr):

        @pl.when(core_zero)
        def _():
            drain(send_buf.at[pl.ds(0, 31)], sem)

        @pl.when(core == 1)
        def _():
            drain(send_buf, sem)


def body(
    queries,
    key_heads,
    value_heads,
    residual,
    out_proj,
    norm_gain,
    routes,
    combine_weight,
    gate_up,
    down_proj,
):
    vmem = pl.BlockSpec(memory_space=pltpu.VMEM)
    hbm = pl.BlockSpec(memory_space=pl.ANY)
    dma = pltpu.SemaphoreType.DMA
    return pl.pallas_call(
        kernel,
        out_shape=(
            jax.ShapeDtypeStruct((TOK, QUARTER), BF16),
            jax.ShapeDtypeStruct((TOK, QUARTER), BF16),
        ),
        in_specs=[vmem, vmem, vmem, vmem, hbm, vmem, vmem, vmem, hbm, hbm],
        out_specs=(vmem, vmem),
        scratch_shapes=[
            pltpu.VMEM((32, TOK, 256), BF16),
            pltpu.VMEM((1024, HD), BF16),
            pltpu.VMEM((1024, HD), F32),
            pltpu.VMEM((1024, HD), F32),
            pltpu.VMEM((1024, HD), F32),
            pltpu.VMEM((512, HD), BF16),
            pltpu.VMEM((512, HD), BF16),
            pltpu.VMEM((8, TOK), F32),
            pltpu.VMEM((8, TOK), F32),
            pltpu.VMEM((2, TOK, 512), BF16),
            pltpu.VMEM((2, 2, 512, QUARTER), BF16),
            pltpu.VMEM((TOK, QUARTER), BF16),
            pltpu.VMEM((TOK, QUARTER), BF16),
            pltpu.VMEM((2, 8, QUARTER), F32),
            pltpu.VMEM((2, TOK, QUARTER), BF16),
            pltpu.VMEM((4, 8, TOK), F32),
            pltpu.VMEM((2, TOK, 384), BF16),
            pltpu.VMEM((384, TOK), F32),
            pltpu.VMEM((2, 256, 256), BF16),
            pltpu.VMEM((384, HALF), F32),
            pltpu.VMEM((32, SLOT_ROWS, 128), BF16),
            pltpu.VMEM((2, 32, SLOT_ROWS, 128), BF16),
            pltpu.VMEM((GROUP_ROWS, D), BF16),
            pltpu.VMEM((2, 2 * HID, D), BF16),
            pltpu.VMEM((2, HID, D), BF16),
            pltpu.VMEM((GROUPS, GROUP_ROWS, HALF), BF16),
            pltpu.VMEM((GROUPS, GROUP_ROWS, HALF), BF16),
            pltpu.VMEM((GROUPS, GROUP_ROWS, HALF), F32),
            pltpu.VMEM((32, SLOT_ROWS, 128), BF16),
            pltpu.VMEM((32, SLOT_ROWS, 128), BF16),
            pltpu.VMEM((384, HALF), BF16),
            pltpu.VMEM((TOK, QUARTER), BF16),
            pltpu.VMEM((TOK, QUARTER), BF16),
            dma((16,)),
            dma((4,)),
            dma((32,)),
            dma((32,)),
            dma((GROUPS,)),
            dma((GROUPS,)),
            dma((32,)),
            dma,
            dma,
            dma,
            dma,
            dma,
            dma((11,)),
            dma((11,)),
            dma((4,)),
            dma((4,)),
            dma((4,)),
            pltpu.SemaphoreType.REGULAR,
        ],
        compiler_params=pltpu.CompilerParams(
            collective_id=0,
            has_side_effects=True,
            vmem_limit_bytes=58 * 1024 * 1024,
        ),
        cost_estimate=pl.CostEstimate(
            flops=8_000_000_000, bytes_accessed=20_000_000, transcendentals=5_000_000
        ),
    )(
        queries,
        key_heads,
        value_heads,
        residual,
        out_proj,
        norm_gain,
        routes.T,
        combine_weight.T,
        gate_up.reshape(D, 2 * HID).T,
        down_proj.reshape(HID, D),
    )


def solution(mesh):
    placed = (
        P("seq", "head"),
        P("seq", "head"),
        P("seq", "head"),
        P("seq", "head"),
        P("head", None),
        P("head"),
        P("seq", None),
        P("seq", None),
        P("seq", None, None, "head"),
        P("seq", "head", None),
    )
    return jax.shard_map(
        body,
        mesh=mesh,
        in_specs=placed,
        out_specs=(P("seq", "head"), P("seq", "head")),
        check_vma=False,
    )
```

```python
import math

import jax
import jax.numpy as jnp
from jax import lax
from jax.experimental import pallas as pl
from jax.experimental.pallas import tpu as pltpu
from jax.sharding import PartitionSpec as P

D = 3584
HD = 128
TOK = 128
QUARTER = 896
HALF = 1792
HID = 320
SLOT_ROWS = 144
GROUP = 8
GROUPS = 4
GROUP_ROWS = 80
EPSILON = 1e-06
SCALE2 = math.log2(math.e) / math.sqrt(HD)
MESH = pl.DeviceIdType.MESH
F32 = jnp.float32
BF16 = jnp.bfloat16


def dot(a, b):
    return jnp.dot(a, b, preferred_element_type=F32)


def dot_nt(a, b):
    return lax.dot_general(a, b, (((1,), (1,)), ((), ())), preferred_element_type=F32)


def iota(shape, dim):
    return lax.broadcasted_iota(jnp.int32, shape, dim)


def kernel(
    q_ref,
    k_ref,
    v_ref,
    residual_ref,
    out_proj_ref,
    gain_ref,
    routes_ref,
    weight_ref,
    gate_up_ref,
    down_ref,
    both_ref,
    kv,
    qr,
    acc,
    row_max,
    row_sum,
    part_send,
    part_recv,
    stat_send,
    stat_recv,
    att,
    wo,
    rs_send,
    rs_recv,
    gains,
    mid_half,
    squares,
    wc,
    onehot,
    perm,
    ymat,
    send_buf,
    xbuf,
    xmat,
    gu,
    wd,
    po_send,
    po_recv,
    po_own,
    ret_send,
    ret,
    rmat,
    comb_send,
    comb_recv,
    ra,
    rb,
    rd,
    rp,
    rpo,
    spo,
    rr,
    sa,
    sb,
    sd,
    sp,
    sr,
    misc_send,
    misc_recv,
    weight_send,
    weight_recv,
    weight_local,
    column,
):
    seq, head = lax.axis_index("seq"), lax.axis_index("head")
    y, z = lax.div(seq, 16), lax.rem(seq, 8)
    xh = lax.rem(lax.div(seq, 8), 2)
    xl, core = lax.div(head, 2), lax.rem(head, 2)
    other = 1 - core
    core_zero = core == 0
    my_kv = z * 4 + y
    my_j = y * 8 + z
    far_h, far_l = (xh + core) % 2, (xl + core) % 2
    half_in = far_l

    def dev(y_, xh_, z_, xl_, core_):
        return {"seq": (y_ * 2 + xh_) * 8 + z_, "head": xl_ * 2 + core_}

    partner = dev(y, xh, z, xl, other)
    pair = dev(y, xh, z, 1 - xl, core)
    diagonal = dev(y, xh, z, 1 - xl, other)
    twin = dev(y, 1 - xh, z, xl, core)
    cross = dev(y, 1 - xh, z, 1 - xl, core)

    def wrap(a, n):
        return lax.rem(a + n, n)

    yp, ym, y2 = wrap(y + 1, 4), wrap(y - 1, 4), wrap(y + 2, 4)
    zp, zm = wrap(z + 1, 8), wrap(z - 1, 8)

    def far(j):
        return dev(lax.div(j, 8), far_h, lax.rem(j, 8), far_l, core)

    barrier = pltpu.get_barrier_semaphore()

    def greet(device):
        pl.semaphore_signal(barrier, inc=1, device_id=device, device_id_type=MESH)

    for device in (
        dev(yp, xh, z, xl, core),
        dev(ym, xh, z, xl, core),
        dev(y2, xh, z, xl, core),
        dev(y, xh, zp, xl, core),
        dev(y, xh, zm, xl, core),
        twin,
        partner,
        pair,
        diagonal,
        cross,
    ):
        greet(device)

    for j in range(4):
        qr[j * TOK : (j + 1) * TOK, :] = q_ref[:, j * HD : (j + 1) * HD]
    kv[my_kv, :, 0:128] = k_ref[...]
    kv[my_kv, :, 128:256] = v_ref[...]
    gains[core, :, :] = jnp.broadcast_to(gain_ref[...].astype(F32).reshape(1, QUARTER), (8, QUARTER))
    pl.semaphore_wait(barrier, 10)

    def rcopy(src, dst, send, recv, device):
        return pltpu.make_async_remote_copy(
            src_ref=src,
            dst_ref=dst,
            send_sem=send,
            recv_sem=recv,
            device_id=device,
            device_id_type=MESH,
        )

    def y_block(yb):
        return kv.at[z * 4 + yb]

    def bundle(zb, h):
        return kv.at[pl.ds(zb * 4 + h * 2, 2)]

    def send_bundle(zb, h, to):
        part = bundle(zb, h)
        rcopy(part, part, sa, ra.at[zb * 2 + h], dev(y, xh, to, xl, core)).start()

    def wait_bundle(zb, h):
        part = bundle(zb, h)
        pltpu.make_async_copy(part, part, ra.at[zb * 2 + h]).wait()

    near = y + 1 - 2 * lax.rem(y, 2)
    others = (near, lax.rem(near + 2, 4), y2)
    for yb in others:
        rcopy(y_block(y), y_block(y), sb, rb.at[y], dev(yb, xh, z, xl, core)).start()
    q_copy = rcopy(
        qr.at[pl.ds(0, 512)], qr.at[pl.ds(512, 512)], misc_send.at[0], misc_recv.at[0], twin
    )
    q_copy.start()
    gain_copy = rcopy(gains.at[core], gains.at[core], misc_send.at[1], misc_recv.at[1], partner)
    gain_copy.start()

    h_near = lax.div(y, 2)
    for h, sources in ((h_near, others[0:1]), (1 - h_near, others[1:3])):
        for yb in sources:
            pltpu.make_async_copy(y_block(yb), y_block(yb), rb.at[yb]).wait()
        send_bundle(z, h, zp)
        send_bundle(z, h, zm)

    wo_copies = []
    for hf in range(2):
        mine = pl.ds(pl.multiple_of((hf * 2 + core) * QUARTER, 128), QUARTER)
        theirs = pl.ds(pl.multiple_of((hf * 2 + other) * QUARTER, 128), QUARTER)
        wo_copies.append(
            rcopy(
                out_proj_ref.at[:, theirs],
                wo.at[core, hf],
                weight_send.at[hf],
                weight_recv.at[hf],
                partner,
            )
        )
        wo_copies[-1].start()
        wo_copies.append(
            pltpu.make_async_copy(out_proj_ref.at[:, mine], wo.at[core, hf], weight_local.at[hf])
        )
    for copy in wo_copies[1::2]:
        copy.start()
    ffn_copies = []
    for n, (src, dst) in enumerate(((gate_up_ref, gu), (down_ref, wd))):
        remote = rcopy(
            src, dst.at[core], weight_send.at[2 + n], weight_recv.at[2 + n], partner
        )
        local = pltpu.make_async_copy(src, dst.at[core], weight_local.at[2 + n])
        remote.start()
        local.start()
        ffn_copies += [remote, local]

    acc[...] = jnp.zeros((1024, HD), F32)
    row_sum[...] = jnp.zeros((1024, HD), F32)
    row_max[...] = jnp.full((1024, HD), -1e30, F32)

    eye = iota((TOK, TOK), 0) == iota((TOK, TOK), 1)

    def to_row(column):
        return jnp.sum(jnp.where(eye, column, 0.0), axis=0, keepdims=True)

    def to_column(row):
        return jnp.sum(jnp.where(eye, row, 0.0), axis=1, keepdims=True)

    lane = iota((1, 384), 1)
    main = lane < 256
    extra = lane - 256
    j_row = jnp.where(main, lax.shift_right_logical(lane, 3), lax.shift_right_logical(jnp.maximum(extra, 0), 1))
    s_row = jnp.where(main, lane & 7, 8 + (extra & 1))
    e_row = lax.shift_right_logical(j_row, 3) * 16 + far_h * 8 + (j_row & 7)
    e_row = jnp.where(j_row < 32, e_row, -1).astype(F32)
    named = jnp.zeros((TOK, 384), F32)
    weight = jnp.zeros((TOK, 384), F32)
    for k in range(4):
        same = to_column(routes_ref[k : k + 1, :].astype(F32)) == e_row
        named = jnp.where(same, 1.0, named)
        weight = jnp.where(same, to_column(weight_ref[k : k + 1, :]), weight)
    earlier = jnp.where(iota((TOK, TOK), 1) < iota((TOK, TOK), 0), 1.0, 0.0).astype(BF16)
    count = dot(earlier, named.astype(BF16))
    taken = jnp.where(count == s_row.astype(F32), named, 0.0)
    weight = weight * taken
    high = weight.astype(BF16)
    wc[0] = high
    wc[1] = (weight - high.astype(F32)).astype(BF16)
    onehot[...] = taken.T
    for which in range(2):
        o, i = iota((256, 256), which), iota((256, 256), 1 - which)
        rem = o & 31
        source = lax.shift_right_logical(rem, 1) * 16 + lax.shift_right_logical(o, 5) * 2 + (rem & 1)
        perm[which] = jnp.where((source == i) & (rem < 28), 1.0, 0.0).astype(BF16)
    rmat[...] = jnp.zeros((384, HALF), BF16)

    def flash(zb, first, count):
        block = kv[pl.ds(zb * 4, 4)]
        keys = block[:, :, 0:128].reshape(512, HD)
        values = block[:, :, 128:256].reshape(512, HD)

        def tile(t, carry):
            rows = pl.ds(pl.multiple_of(first + t * 256, 256), 256)
            scores = dot_nt(qr[rows, :], keys)
            old = row_max[rows, :]
            new = jnp.maximum(old, jnp.max(scores, axis=1, keepdims=True))
            p = jnp.exp2((scores - new[:, 0:1]) * SCALE2)
            fade = jnp.exp2((old - new) * SCALE2)
            lanes = (p[:, 0:128] + p[:, 128:256]) + (p[:, 256:384] + p[:, 384:512])
            row_sum[rows, :] = row_sum[rows, :] * fade + lanes
            acc[rows, :] = acc[rows, :] * fade + dot(p.astype(BF16), values)
            row_max[rows, :] = new
            return carry

        lax.fori_loop(0, count // 256, tile, 0)

    def step(d, carry):
        ahead, behind = wrap(z - d, 8), wrap(z + d, 8)
        for h in (h_near, 1 - h_near):
            wait_bundle(ahead, h)

            @pl.when((d < 3) | (h == 0))
            def _():
                send_bundle(ahead, h, zp)

            wait_bundle(behind, h)

            @pl.when((d < 3) | (h == 1))
            def _():
                send_bundle(behind, h, zm)

        flash(ahead, 0, 1024)
        flash(behind, 0, 1024)
        return carry

    q_copy.wait_recv()
    flash(z, 0, 1024)
    lax.fori_loop(1, 4, step, 0)
    zf = wrap(z + 4, 8)
    for h in range(2):
        wait_bundle(zf, h)

    @pl.when(core == 1)
    def _():
        pl.semaphore_signal(column, inc=1, device_id=cross, device_id_type=MESH)

    flash(zf, 512, 512)
    for j in range(4):
        rows = pl.ds(512 + j * TOK, TOK)
        total = jnp.sum(row_sum[rows, :], axis=1, keepdims=True)
        part_send[j * TOK : (j + 1) * TOK, :] = (acc[rows, :] / total).astype(BF16)
        stat_send[j : j + 1, :] = to_row(row_max[rows, :] * SCALE2 + jnp.log2(total))
    stat_send[4:8, :] = jnp.zeros((4, TOK), F32)
    part_copy = rcopy(part_send, part_recv, misc_send.at[2], misc_recv.at[2], twin)
    stat_copy = rcopy(stat_send, stat_recv, misc_send.at[3], misc_recv.at[3], twin)
    part_copy.start()
    stat_copy.start()
    flash(zf, 0, 512)
    part_copy.wait_recv()
    stat_copy.wait_recv()
    for j in range(4):
        rows = slice(j * TOK, (j + 1) * TOK)
        total = jnp.sum(row_sum[rows, :], axis=1, keepdims=True)
        own = acc[rows, :] / total
        own_stat = row_max[rows, :] * SCALE2 + jnp.log2(total)
        their_stat = to_column(stat_recv[j : j + 1, :])
        own_share = 1.0 / (1.0 + jnp.exp2(their_stat - own_stat))
        their_share = 1.0 / (1.0 + jnp.exp2(own_stat - their_stat))
        att[core, :, rows] = (
            own * own_share + part_recv[rows, :].astype(F32) * their_share
        ).astype(BF16)
    att_copy = rcopy(att.at[core], att.at[core], misc_send.at[4], misc_recv.at[4], partner)
    att_copy.start()
    for copy in wo_copies[0::2]:
        copy.wait_recv()
    for copy in wo_copies[1::2]:
        copy.wait()
    gain_copy.wait_recv()
    att_copy.wait_recv()

    def project(hf):
        return dot(att[0], wo[0, hf]) + dot(att[1], wo[1, hf])

    rs_send[...] = project(1 - xl).astype(BF16)
    rs_copy = rcopy(rs_send, rs_recv, misc_send.at[5], misc_recv.at[5], pair)
    rs_copy.start()
    own = project(xl) + residual_ref[...].astype(F32)
    rs_copy.wait_recv()
    middle = (own + rs_recv[...].astype(F32)).astype(BF16)
    mid_half[core, :, :] = middle
    mid_copy = rcopy(
        mid_half.at[core], mid_half.at[core], misc_send.at[6], misc_recv.at[6], partner
    )
    mid_copy.start()
    both_ref[0:TOK, :] = middle
    mid_float = middle.astype(F32)
    squares[head] = jnp.broadcast_to(
        to_row(jnp.sum(mid_float * mid_float, axis=1, keepdims=True)), (8, TOK)
    )
    square_copies = [
        rcopy(squares.at[head], squares.at[head], misc_send.at[7 + n], misc_recv.at[7 + n], device)
        for n, device in enumerate((partner, pair, diagonal))
    ]
    for copy in square_copies:
        copy.start()
    mid_copy.wait_recv()
    hot = onehot[...]
    hot16 = hot.astype(BF16)
    for c in range(2):
        ymat[:, c * QUARTER : (c + 1) * QUARTER] = dot(hot16, mid_half[c])
    for copy in square_copies:
        copy.wait_recv()
    total = squares[0, 0:1] + squares[1, 0:1] + squares[2, 0:1] + squares[3, 0:1]
    inverse = lax.rsqrt(total / D + EPSILON)
    row_scale = jnp.sum(hot * inverse, axis=1, keepdims=True)

    def lane_block(c):
        return slice(c * 128, (c + 1) * 128)

    def scaled(rows, c):
        q, inner = c // 7, c % 7
        return ymat[rows, lane_block(c)] * row_scale[rows] * gains[q, 0:1, lane_block(inner)]

    for c in range(0, 14, 2):
        both = [scaled(slice(0, 256), c + n).reshape(32, 8, 128) for n in range(2)]
        send_buf[:, c * 8 : c * 8 + 16, :] = jnp.concatenate(both, axis=1).astype(BF16)
    for g in range(4):
        rows = slice(256 + 16 * g, 272 + 16 * g)
        stack = jnp.concatenate(
            [scaled(rows, c).astype(BF16) for c in range(14)] + [jnp.zeros((32, 128), BF16)], axis=0
        )
        send_buf[8 * g : 8 * g + 8, 112:144, :] = (
            dot(perm[0], stack).reshape(8, 32, 128).astype(BF16)
        )

    def exchange(buffer, place, send, recv, first, count):
        def one(i, carry):
            j = lax.rem(my_j + i, 32)
            rcopy(buffer.at[j], place(), send, recv.at[my_j], far(j)).start()
            return carry

        lax.fori_loop(first, count, one, 0)

    def landing():
        return xbuf.at[xl, my_j]

    @pl.when(core == 1)
    def _():
        pl.semaphore_wait(column, 1)

    @pl.when(core_zero)
    def _():
        pltpu.make_async_copy(send_buf.at[my_j], xbuf.at[xl, my_j], rd.at[my_j]).start()

    @pl.when(core == 1)
    def _():
        rcopy(send_buf.at[my_j], landing(), sd, rd.at[my_j], far(my_j)).start()

    exchange(send_buf, landing, sd, rd, 1, 32)

    for copy in ffn_copies[0::2]:
        copy.wait_recv()
    for copy in ffn_copies[1::2]:
        copy.wait()

    def source(i):
        return wrap(my_j - i, 32)

    def forward(g):
        def one(n, carry):
            s = source(g * GROUP + n)
            block = xbuf.at[half_in, s]
            pltpu.make_async_copy(block, block, rd.at[s]).wait()
            rcopy(block, block, sp, rp.at[s], pair).start()
            return carry

        lax.fori_loop(0, GROUP, one, 0)

    def gather_rows(g):
        def await_pair(n, carry):
            s = source(g * GROUP + n)
            block = xbuf.at[1 - half_in, s]
            pltpu.make_async_copy(block, block, rp.at[s]).wait()
            return carry

        lax.fori_loop(0, GROUP, await_pair, 0)
        for half in range(2):
            for p in range(GROUP // 2):
                both = [
                    xbuf[half, source(g * GROUP + 2 * p + n), 0:112, :]
                    .astype(F32)
                    .reshape(14, 8, 128)
                    for n in range(2)
                ]
                rows = jnp.concatenate(both, axis=1).astype(BF16)
                for c in range(14):
                    xmat[16 * p : 16 * p + 16, lane_block(half * 14 + c)] = rows[c]
            stack = jnp.concatenate(
                [xbuf[half, source(g * GROUP + n), 112:144, :] for n in range(GROUP)], axis=0
            )
            rows = dot(perm[1], stack).astype(BF16)
            for c in range(14):
                xmat[64:80, lane_block(half * 14 + c)] = rows[16 * c : 16 * c + 16]

    def experts(g):
        x = xmat[...]
        parts = []
        for c in range(2):
            gate, up = dot_nt(x, gu[c, 0:HID]), dot_nt(x, gu[c, HID : 2 * HID])
            parts.append((gate / (1.0 + jnp.exp(-gate)) * up).astype(BF16))

        def result(half, n):
            columns = pl.ds(pl.multiple_of(half * HALF + n * QUARTER, 128), QUARTER)
            return dot(parts[0], wd[0, :, columns]) + dot(parts[1], wd[1, :, columns])

        for n in range(2):
            po_send[g, :, n * QUARTER : (n + 1) * QUARTER] = result(1 - half_in, n).astype(BF16)
        rcopy(po_send.at[g], po_recv.at[g], spo.at[g], rpo.at[g], pair).start()
        for n in range(2):
            po_own[g, :, n * QUARTER : (n + 1) * QUARTER] = result(half_in, n)

    def give_back(g):
        pltpu.make_async_copy(po_recv.at[g], po_recv.at[g], rpo.at[g]).wait()
        first = pl.multiple_of(g * GROUP, GROUP)

        def summed(rows, c):
            return po_own[g, rows, lane_block(c)] + po_recv[g, rows, lane_block(c)].astype(F32)

        for c in range(0, 14, 2):
            both = [summed(slice(0, 64), c + n).reshape(8, 8, 128) for n in range(2)]
            ret_send[pl.ds(first, 8), c * 8 : c * 8 + 16, :] = jnp.concatenate(both, axis=1).astype(
                BF16
            )
        stack = jnp.concatenate(
            [summed(slice(64, 80), c).astype(BF16) for c in range(14)]
            + [jnp.zeros((32, 128), BF16)],
            axis=0,
        )
        ret_send[pl.ds(first, 8), 112:144, :] = dot(perm[0], stack).reshape(8, 32, 128).astype(BF16)

        def one(n, carry):
            i = g * GROUP + n
            s = source(i)

            @pl.when(core_zero & (i == 0))
            def _():
                pltpu.make_async_copy(ret_send.at[i], ret.at[my_j], rr.at[my_j]).start()

            @pl.when(jnp.logical_not(core_zero & (i == 0)))
            def _():
                rcopy(ret_send.at[i], ret.at[my_j], sr, rr.at[my_j], far(s)).start()

            return carry

        lax.fori_loop(0, GROUP, one, 0)

    forward(0)

    def turn(g, carry):
        @pl.when(g < GROUPS - 1)
        def _():
            forward(g + 1)

        @pl.when((g > 0) & (g < GROUPS - 1))
        def _():
            give_back(g - 1)

        gather_rows(g)
        experts(g)
        return carry

    lax.fori_loop(0, GROUPS, turn, 0)

    def last(g, carry):
        give_back(g)
        return carry

    lax.fori_loop(GROUPS - 2, GROUPS, last, 0)

    def take_back(n, carry):
        p = lax.rem(lax.div(my_j, 2) + n, 16)
        for m in range(2):
            j = p * 2 + m
            pltpu.make_async_copy(ret.at[j], ret.at[j], rr.at[j]).wait()
        both = [ret[p * 2 + m, 0:112, :].astype(F32).reshape(14, 8, 128) for m in range(2)]
        taken = jnp.concatenate(both, axis=1).astype(BF16)
        rows = pl.ds(pl.multiple_of(p * 16, 16), 16)
        for c in range(14):
            rmat[rows, lane_block(c)] = taken[c]
        return carry

    lax.fori_loop(1, 17, take_back, 0)
    for g in range(4):
        stack = ret[8 * g : 8 * g + 8, 112:144, :].reshape(256, 128)
        rows = dot(perm[1], stack).astype(BF16)
        for c in range(14):
            rmat[256 + 16 * g : 272 + 16 * g, lane_block(c)] = rows[16 * c : 16 * c + 16]

    def combined(which):
        columns = pl.ds(pl.multiple_of(which * QUARTER, 128), QUARTER)
        rows = rmat[:, columns]
        return dot(wc[0], rows) + dot(wc[1], rows)

    comb_send[...] = combined(other).astype(BF16)
    comb_copy = rcopy(comb_send, comb_recv, misc_send.at[10], misc_recv.at[10], partner)
    comb_copy.start()
    own = combined(core)
    comb_copy.wait_recv()
    both_ref[TOK : 2 * TOK, :] = (own + comb_recv[...].astype(F32)).astype(BF16)

    for copy in (
        [q_copy, gain_copy, part_copy, stat_copy, att_copy, rs_copy, mid_copy, comb_copy]
        + square_copies
        + wo_copies[0::2]
        + ffn_copies[0::2]
    ):
        copy.wait_send()
    for g in range(GROUPS):
        pltpu.make_async_copy(po_send.at[g], po_send.at[g], spo.at[g]).wait()

    def drain(ref, sem):
        pltpu.make_async_copy(ref, ref, sem).wait()

    drain(kv.at[pl.ds(0, 28)], sa)
    drain(kv.at[pl.ds(0, 3)], sb)
    drain(xbuf.at[0], sp)
    for sem in (sd, sr):

        @pl.when(core_zero)
        def _():
            drain(send_buf.at[pl.ds(0, 31)], sem)

        @pl.when(core == 1)
        def _():
            drain(send_buf, sem)


def body(
    queries,
    key_heads,
    value_heads,
    residual,
    out_proj,
    norm_gain,
    routes,
    combine_weight,
    gate_up,
    down_proj,
):
    vmem = pl.BlockSpec(memory_space=pltpu.VMEM)
    hbm = pl.BlockSpec(memory_space=pl.ANY)
    dma = pltpu.SemaphoreType.DMA
    both = pl.pallas_call(
        kernel,
        out_shape=jax.ShapeDtypeStruct((2 * TOK, QUARTER), BF16),
        in_specs=[vmem, vmem, vmem, vmem, hbm, vmem, vmem, vmem, hbm, hbm],
        out_specs=vmem,
        scratch_shapes=[
            pltpu.VMEM((32, TOK, 256), BF16),
            pltpu.VMEM((1024, HD), BF16),
            pltpu.VMEM((1024, HD), F32),
            pltpu.VMEM((1024, HD), F32),
            pltpu.VMEM((1024, HD), F32),
            pltpu.VMEM((512, HD), BF16),
            pltpu.VMEM((512, HD), BF16),
            pltpu.VMEM((8, TOK), F32),
            pltpu.VMEM((8, TOK), F32),
            pltpu.VMEM((2, TOK, 512), BF16),
            pltpu.VMEM((2, 2, 512, QUARTER), BF16),
            pltpu.VMEM((TOK, QUARTER), BF16),
            pltpu.VMEM((TOK, QUARTER), BF16),
            pltpu.VMEM((2, 8, QUARTER), F32),
            pltpu.VMEM((2, TOK, QUARTER), BF16),
            pltpu.VMEM((4, 8, TOK), F32),
            pltpu.VMEM((2, TOK, 384), BF16),
            pltpu.VMEM((384, TOK), F32),
            pltpu.VMEM((2, 256, 256), BF16),
            pltpu.VMEM((384, HALF), F32),
            pltpu.VMEM((32, SLOT_ROWS, 128), BF16),
            pltpu.VMEM((2, 32, SLOT_ROWS, 128), BF16),
            pltpu.VMEM((GROUP_ROWS, D), BF16),
            pltpu.VMEM((2, 2 * HID, D), BF16),
            pltpu.VMEM((2, HID, D), BF16),
            pltpu.VMEM((GROUPS, GROUP_ROWS, HALF), BF16),
            pltpu.VMEM((GROUPS, GROUP_ROWS, HALF), BF16),
            pltpu.VMEM((GROUPS, GROUP_ROWS, HALF), F32),
            pltpu.VMEM((32, SLOT_ROWS, 128), BF16),
            pltpu.VMEM((32, SLOT_ROWS, 128), BF16),
            pltpu.VMEM((384, HALF), BF16),
            pltpu.VMEM((TOK, QUARTER), BF16),
            pltpu.VMEM((TOK, QUARTER), BF16),
            dma((16,)),
            dma((4,)),
            dma((32,)),
            dma((32,)),
            dma((GROUPS,)),
            dma((GROUPS,)),
            dma((32,)),
            dma,
            dma,
            dma,
            dma,
            dma,
            dma((11,)),
            dma((11,)),
            dma((4,)),
            dma((4,)),
            dma((4,)),
            pltpu.SemaphoreType.REGULAR,
        ],
        compiler_params=pltpu.CompilerParams(
            collective_id=0,
            has_side_effects=True,
            vmem_limit_bytes=58 * 1024 * 1024,
        ),
        cost_estimate=pl.CostEstimate(
            flops=8_000_000_000, bytes_accessed=20_000_000, transcendentals=5_000_000
        ),
    )(
        queries,
        key_heads,
        value_heads,
        residual,
        out_proj,
        norm_gain,
        routes.T,
        combine_weight.T,
        gate_up.reshape(D, 2 * HID).T,
        down_proj.reshape(HID, D),
    )
    return both[0:TOK], both[TOK : 2 * TOK]


def solution(mesh):
    placed = (
        P("seq", "head"),
        P("seq", "head"),
        P("seq", "head"),
        P("seq", "head"),
        P("head", None),
        P("head"),
        P("seq", None),
        P("seq", None),
        P("seq", None, None, "head"),
        P("seq", "head", None),
    )
    return jax.shard_map(
        body,
        mesh=mesh,
        in_specs=placed,
        out_specs=(P("seq", "head"), P("seq", "head")),
        check_vma=False,
    )
```
